512 devices in a mesh: front: 16 (over y_lo, x, core), row: 4 (over y_hi), col: 8 (over z).
Axes of the slice: x: 4, y: 8 (y_hi: 4, y_lo: 2; y = y_hi * 2 + y_lo), z: 8, core: 2. Of those that a mesh axis runs over, the one named last changes fastest.
Arguments:
- assembled: float32 [16, 4096, 4096], P('front', ('row', 'col')), may hold values from -6 to 6
- update: bfloat16 [16, 1536, 1536], P('front', ('row', 'col')), may hold values from -6 to 6
- blocks: int32 [16, 12], P('front'), may hold values from 16 to 31, as said below
- inverses: bfloat16 [16, 2, 512, 512], P('front'), as said below
Outputs:
- factor: bfloat16 [16, 4096, 1024], P('front', ('row', 'col'))
- schur: float32 [16, 4096, 3072], P('front', ('row', 'col'))
The draws below stay inside these ranges and needn't reach their ends.
Inputs may be any that keep to these rules, and one draw needn't show every extreme that they name: `blocks`: for each front the entries are strictly increasing, the first is 16 and the last 31. `inverses`: each 512 x 512 matrix is upper triangular.
All inputs are finite; a program needn't handle non-finite values.
Results may differ from the reference program's by a relative error of at most 0.0034.
Values may be sent and summed in bfloat16 or wider, within the bound.
No kernel may reach another device: no remote copies, remote signals or barrier semaphores. Data moves between devices by JAX's collectives and lax.ppermute only.
A program may use at most 64 MiB of HBM per device.

```python
import math
import jax
import jax.numpy as jnp
from jax import lax

ORDER = 4096
PANEL = 512
CHILD = 1536
BLOCK = 128
FRONTS = 16
PARENT_BLOCKS = 32
CHILD_BLOCKS = 12


def draw_blocks(key, part):
    key = jax.random.fold_in(key, 11)
    keys = jax.random.split(key, FRONTS)
    half = PARENT_BLOCKS // 2

    def single(front_key):
        middle = jax.random.permutation(front_key, half - 2)[:CHILD_BLOCKS - 2] + half + 1
        middle = jnp.sort(middle).astype(jnp.int32)
        start = jnp.full((1,), half, jnp.int32)
        finish = jnp.full((1,), PARENT_BLOCKS - 1, jnp.int32)
        return jnp.concatenate([start, middle, finish])
    return jax.vmap(single)(keys).astype(jnp.int32)


def draw_inverses(key, part):
    key = jax.random.fold_in(key, 23)
    diag_key, off_key = jax.random.split(key)
    root = math.sqrt(PANEL)
    shape = (FRONTS, 2, PANEL, PANEL)
    diagonal = jax.random.uniform(diag_key, shape[:-1], jnp.float32, 1.0, 2.4) / root
    spread = jax.random.normal(off_key, shape, jnp.float32) * (0.11 / root)
    upper = jnp.triu(spread, 1) + diagonal[..., None] * jnp.eye(PANEL, dtype=jnp.float32)
    return upper.astype(jnp.bfloat16)


def shard_levels(own_key, extent, shards, smallest, top_value):
    loudness = 1.0
    for position, shards_of in shards:
        draws = jax.random.uniform(jax.random.fold_in(jax.random.fold_in(own_key, 6), position), (shards_of,), jnp.float32, smallest / len(shards), top_value / len(shards))
        loudness = loudness * jnp.repeat(jnp.exp(draws), extent[position] // shards_of).reshape((-1,) + (1,) * (len(extent) - 1 - position))
    return loudness


def gaussian(key, dims, scale, bound, cuts=(), kind=jnp.bfloat16):
    array = scale * jax.random.normal(key, dims, jnp.float32)
    if cuts:
        array = array * shard_levels(key, dims, cuts, -0.22, 0.18)
    return jnp.clip(array, -bound, bound).astype(kind)


def setup_inputs(seed: int = 0) -> dict:
    arg_keys = jax.random.split(jax.random.key(seed), 5)
    return {
        "assembled": gaussian(arg_keys[0], (FRONTS, ORDER, ORDER), 1.0, 6.0, ((0, 16), (1, 32)), jnp.float32),
        "update": gaussian(arg_keys[1], (FRONTS, CHILD, CHILD), 1.0, 6.0, ((0, 16), (1, 32))),
        "blocks": draw_blocks(jax.random.fold_in(arg_keys[4], 71), 0),
        "inverses": draw_inverses(jax.random.fold_in(arg_keys[4], 71), 0),
    }


def one_front(pieces):
    assembled, update, blocks, inverses = pieces
    offsets = jnp.arange(BLOCK, dtype=jnp.int32)
    targets = (blocks[:, None] * BLOCK + offsets[None, :]).reshape(-1).astype(jnp.int32)
    placed = jnp.zeros((ORDER, ORDER), jnp.float32).at[targets[:, None], targets[None, :]].set(update.astype(jnp.float32))
    frontal = assembled + placed
    inverse_one = inverses[0].astype(jnp.float32)
    inverse_two = inverses[1].astype(jnp.float32)
    first = jnp.dot(frontal[:, :PANEL], inverse_one, precision=lax.Precision.HIGHEST, preferred_element_type=jnp.float32).astype(jnp.bfloat16)
    second = frontal[:, PANEL:] - jnp.dot(first, first[PANEL:].T, preferred_element_type=jnp.float32)
    positions = jnp.arange(ORDER, dtype=jnp.int32)
    raw_panel = jnp.dot(second[:, :PANEL], inverse_two, precision=lax.Precision.HIGHEST, preferred_element_type=jnp.float32)
    panel = jnp.where(positions[:, None] >= PANEL, raw_panel, jnp.zeros_like(raw_panel)).astype(jnp.bfloat16)
    schur = second[:, PANEL:] - jnp.dot(panel, panel[2 * PANEL:].T, preferred_element_type=jnp.float32)
    return jnp.concatenate([first, panel], axis=1), schur


def reference(assembled, update, blocks, inverses):
    sibling = update.reshape(FRONTS // 2, 2, CHILD, CHILD)[:, ::-1].reshape(FRONTS, CHILD, CHILD)
    factor, schur = lax.map(one_front, (assembled, sibling, blocks, inverses))
    return factor, schur
```

```python
import jax
import jax.numpy as jnp
from jax import lax
from jax.experimental import pallas as pl
from jax.experimental.pallas import tpu as pltpu
from jax.sharding import PartitionSpec as P

WIDTH = 512
ROWS = 128
GROUP = 1024
CHILD = 1536
CHILD_BLOCKS = 12
CHILD_ROWS = 48
VMEM_LIMIT = 48 * 1024 * 1024

F32 = jnp.float32
BF16 = jnp.bfloat16


def dot(a, b):
    return jnp.dot(a, b, preferred_element_type=F32)


def dot_t(a, b):
    return lax.dot_general(a, b, (((1,), (1,)), ((), ())), preferred_element_type=F32)


def dot_split(a, b, terms):
    total = None
    for _ in range(terms):
        part = a.astype(BF16)
        a = a - part.astype(F32)
        product = dot(part, b)
        total = product if total is None else total + product
    return total


def first_kernel(front_ref, inverse_ref, both_ref, first_ref, next_ref):
    first = dot_split(front_ref[0, :, :WIDTH], inverse_ref[0, 0], 3).astype(BF16)
    following = front_ref[0, :, WIDTH:].astype(BF16)
    first_ref[...] = first
    next_ref[...] = following
    both_ref[:, :WIDTH] = first
    both_ref[:, WIDTH:] = following


def first_panel(assembled, inverses):
    return pl.pallas_call(
        first_kernel,
        grid=(1,),
        in_specs=[
            pl.BlockSpec((1, ROWS, 2 * WIDTH), lambda i: (0, 0, 0)),
            pl.BlockSpec((1, 1, WIDTH, WIDTH), lambda i: (0, 0, 0, 0)),
        ],
        out_specs=[
            pl.BlockSpec((ROWS, 2 * WIDTH), lambda i: (0, 0)),
            pl.BlockSpec((ROWS, WIDTH), lambda i: (0, 0)),
            pl.BlockSpec((ROWS, WIDTH), lambda i: (0, 0)),
        ],
        out_shape=[
            jax.ShapeDtypeStruct((ROWS, 2 * WIDTH), BF16),
            jax.ShapeDtypeStruct((ROWS, WIDTH), BF16),
            jax.ShapeDtypeStruct((ROWS, WIDTH), BF16),
        ],
        compiler_params=pltpu.CompilerParams(vmem_limit_bytes=VMEM_LIMIT),
        name="first_panel",
    )(assembled, inverses)


def piece_of(z):
    return jnp.where(z < 4, z ^ 1, z - 4)


def product_kernel(
    where_ref, front_ref, inverse_ref, first_ref, firsts_ref, nexts_ref, column_ref,
    mine_ref, beside_ref, across_ref, product_ref, factor_ref, second_ref, rows_ref,
):
    r, z = where_ref[0], where_ref[1]
    other = jnp.where(z % 2 == 1, (z + 1) % 8, (z + 7) % 8)
    here, there = piece_of(z), piece_of(other)

    def put(piece, value):
        second_ref[pl.ds(pl.multiple_of(piece * ROWS, ROWS), ROWS), :] = value

    put(here, mine_ref[...])
    put(here ^ 1, beside_ref[...])
    put(there, across_ref[:ROWS])
    put(there ^ 1, across_ref[ROWS:])
    inverse = inverse_ref[0, 0]

    own = front_ref[0] - dot_t(first_ref[...], second_ref[...])
    own = dot_split(own, inverse, 3)
    own = jnp.where((r == 0) & (z < 4), jnp.zeros_like(own), own)
    factor_ref[0, :, :WIDTH] = first_ref[...]
    factor_ref[0, :, WIDTH:] = own.astype(BF16)

    for k in range(4):
        panel = nexts_ref[k].astype(F32) - dot_t(firsts_ref[k], second_ref[...])
        panel = dot_split(panel, inverse, 2)
        if k == 0:
            panel = jnp.where(z < 4, jnp.zeros_like(panel), panel)
        rows_ref[pl.ds(k * ROWS, ROWS), :WIDTH] = firsts_ref[k]
        rows_ref[pl.ds(k * ROWS, ROWS), WIDTH:] = panel.astype(BF16)

    def column(j, carry):
        first = column_ref[j, :, :WIDTH]
        panel = column_ref[j, :, WIDTH:].astype(F32) - dot_t(first, second_ref[...])
        panel = dot_split(panel, inverse, 2).astype(BF16)
        place = pl.ds(pl.multiple_of(j * ROWS, ROWS), ROWS)
        for k in range(4):
            rows = rows_ref[pl.ds(k * ROWS, ROWS), :]
            total = dot_t(rows[:, :WIDTH], first) + dot_t(rows[:, WIDTH:], panel)
            product_ref[k, :, place] = total.astype(BF16)
        return carry

    lax.fori_loop(0, 8, column, 0)


def products(where, assembled, inverses, first, firsts, nexts, columns, mine, beside, across):
    whole = lambda *shape: pl.BlockSpec(shape, lambda i, w: (0,) * len(shape))
    return pl.pallas_call(
        product_kernel,
        grid_spec=pltpu.PrefetchScalarGridSpec(
            num_scalar_prefetch=1,
            grid=(1,),
            in_specs=[
                pl.BlockSpec((1, ROWS, WIDTH), lambda i, w: (0, 0, 1)),
                pl.BlockSpec((1, 1, WIDTH, WIDTH), lambda i, w: (0, 1, 0, 0)),
                whole(ROWS, WIDTH),
                whole(4, ROWS, WIDTH),
                whole(4, ROWS, WIDTH),
                whole(8, ROWS, 2 * WIDTH),
                whole(ROWS, WIDTH),
                whole(ROWS, WIDTH),
                whole(2 * ROWS, WIDTH),
            ],
            out_specs=[whole(4, ROWS, GROUP), whole(1, ROWS, 2 * WIDTH)],
            scratch_shapes=[
                pltpu.VMEM((WIDTH, WIDTH), BF16),
                pltpu.VMEM((4 * ROWS, 2 * WIDTH), BF16),
            ],
        ),
        out_shape=[
            jax.ShapeDtypeStruct((4, ROWS, GROUP), BF16),
            jax.ShapeDtypeStruct((1, ROWS, 2 * WIDTH), BF16),
        ],
        compiler_params=pltpu.CompilerParams(vmem_limit_bytes=VMEM_LIMIT),
        name="products",
    )(where, assembled, inverses, first, firsts, nexts, columns, mine, beside, across)


PIECES = (
    ((0, 0, 48, 0), (1, 0, 48, 48), (2, 0, 32, 96)),
    ((2, 32, 16, 0), (3, 0, 48, 16), (4, 0, 48, 64), (5, 0, 16, 112)),
    ((5, 16, 32, 0), (6, 0, 48, 32), (7, 0, 48, 80)),
)


def final_kernel(where_ref, front_ref, product_ref, child_ref, schur_ref, block_ref, sems):
    step = pl.program_id(0)
    r, z = where_ref[0], where_ref[1]
    target = r * 8 + z
    found, child = jnp.int32(0), jnp.int32(0)
    for b in range(CHILD_BLOCKS):
        hit = (where_ref[2 + b] == target).astype(jnp.int32)
        found, child = found + hit, child + hit * b
    slot = jnp.clip(r - child // 3, 0, 2)
    turn = child % 3

    def copies(j):
        return [
            pltpu.make_async_copy(
                child_ref.at[z_from, slot, pl.ds(start, rows), :],
                block_ref.at[pl.ds(place, rows), :],
                sems.at[i],
            )
            for i, (z_from, start, rows, place) in enumerate(PIECES[j])
        ]

    for j in range(3):
        @pl.when((step == 0) & (found > 0) & (turn == j))
        def _():
            for copy in copies(j):
                copy.start()

    schur_ref[0] = front_ref[0] - product_ref[0].astype(F32)

    for j in range(3):
        @pl.when((step == 1) & (found > 0) & (turn == j))
        def _():
            for copy in copies(j):
                copy.wait()

    for b in range(CHILD_BLOCKS):
        parent = where_ref[2 + b]
        @pl.when((found > 0) & (step > 0) & (parent // 8 == step + 1))
        def _():
            place = pl.ds(pl.multiple_of((parent % 8) * ROWS, ROWS), ROWS)
            schur_ref[0, :, place] += block_ref[:, b * ROWS : (b + 1) * ROWS].astype(F32)


def final(where, assembled, product, children):
    return pl.pallas_call(
        final_kernel,
        grid_spec=pltpu.PrefetchScalarGridSpec(
            num_scalar_prefetch=1,
            grid=(3,),
            in_specs=[
                pl.BlockSpec((1, ROWS, GROUP), lambda i, w: (0, 0, i + 1)),
                pl.BlockSpec((1, ROWS, GROUP), lambda i, w: (i + 1, 0, 0)),
                pl.BlockSpec(memory_space=pl.ANY),
            ],
            out_specs=pl.BlockSpec((1, ROWS, GROUP), lambda i, w: (0, 0, i)),
            scratch_shapes=[
                pltpu.VMEM((ROWS, CHILD), BF16),
                pltpu.SemaphoreType.DMA((4,)),
            ],
        ),
        out_shape=jax.ShapeDtypeStruct((1, ROWS, 3 * GROUP), F32),
        compiler_params=pltpu.CompilerParams(vmem_limit_bytes=VMEM_LIMIT),
        name="final",
    )(where, assembled, product, children)


def send_child(update):
    received = []
    for distance in range(3):
        pairs = [
            (front * 4 + k, (front ^ 1) * 4 + k + distance)
            for front in range(16)
            for k in range(4)
            if 2 <= k + distance <= 3
        ]
        received.append(lax.ppermute(update[0], ("front", "row"), pairs))
    return jnp.stack(received)


def on_device(assembled, update, blocks, inverses):
    r, z = lax.axis_index("row"), lax.axis_index("col")
    where = jnp.concatenate([jnp.stack([r, z]).astype(jnp.int32), blocks[0]])

    both, first, following = first_panel(assembled, inverses)
    columns = lax.all_gather(both, "col", axis=0)
    firsts = lax.all_gather(first, "row", axis=0)

    top = firsts[0]
    passed = lax.ppermute(top, "col", [(4, 1), (5, 0), (6, 3), (7, 2)])
    mine = jnp.where(z < 4, passed, top)
    beside = lax.ppermute(mine, "col", [(i, i ^ 1) for i in range(8)])
    across = lax.ppermute(
        jnp.concatenate([mine, beside]),
        "col",
        [(i, (i + 1) % 8 if i % 2 else (i + 7) % 8) for i in range(8)],
    )
    nexts = lax.all_gather(following, "row", axis=0)
    arriving = send_child(update)
    arriving, columns = lax.optimization_barrier((arriving, columns))
    children = lax.all_gather(arriving, "col", axis=0)

    product, factor = products(
        where, assembled, inverses, first, firsts, nexts, columns, mine, beside, across
    )
    product = lax.all_to_all(product, "row", 0, 0)
    return factor, final(where, assembled, product, children)


def solution(mesh):
    return jax.shard_map(
        on_device,
        mesh=mesh,
        in_specs=(
            P("front", ("row", "col"), None),
            P("front", ("row", "col"), None),
            P("front", None),
            P("front", None, None, None),
        ),
        out_specs=(P("front", ("row", "col"), None), P("front", ("row", "col"), None)),
        check_vma=False,
    )
```

```python
import jax
import jax.numpy as jnp
from jax import lax
from jax.experimental import pallas as pl
from jax.experimental.pallas import tpu as pltpu
from jax.sharding import PartitionSpec as P

WIDTH = 512
ROWS = 128
GROUP = 1024
CHILD = 1536
CHILD_BLOCKS = 12
CHILD_ROWS = 48
PART_ROWS = ROWS + 3 * CHILD_ROWS
VMEM_LIMIT = 60 * 1024 * 1024

F32 = jnp.float32
BF16 = jnp.bfloat16


def dot(a, b):
    return jnp.dot(a, b, preferred_element_type=F32)


def dot_t(a, b):
    return lax.dot_general(a, b, (((1,), (1,)), ((), ())), preferred_element_type=F32)


def dot_split(a, b, terms):
    total = None
    for _ in range(terms):
        part = a.astype(BF16)
        a = a - part.astype(F32)
        product = dot(part, b)
        total = product if total is None else total + product
    return total


def first_kernel(front_ref, inverse_ref, child_ref, both_ref, first_ref, parts_ref):
    first = dot_split(front_ref[0, :, :WIDTH], inverse_ref[0, 0], 3).astype(BF16)
    following = front_ref[0, :, WIDTH:].astype(BF16)
    both_ref[:, :WIDTH] = first
    both_ref[:, WIDTH:] = following
    first_ref[...] = first
    for k in range(4):
        parts_ref[k, :ROWS] = following
        for part in range(3):
            start = ROWS + part * CHILD_ROWS
            parts_ref[k, start : start + CHILD_ROWS] = child_ref[:, part * WIDTH : (part + 1) * WIDTH]


def first_panel(assembled, inverses, child):
    return pl.pallas_call(
        first_kernel,
        grid=(1,),
        in_specs=[
            pl.BlockSpec((1, ROWS, 2 * WIDTH), lambda i: (0, 0, 0)),
            pl.BlockSpec((1, 1, WIDTH, WIDTH), lambda i: (0, 0, 0, 0)),
            pl.BlockSpec((CHILD_ROWS, CHILD), lambda i: (0, 0)),
        ],
        out_specs=[
            pl.BlockSpec((ROWS, 2 * WIDTH), lambda i: (0, 0)),
            pl.BlockSpec((ROWS, WIDTH), lambda i: (0, 0)),
            pl.BlockSpec((4, PART_ROWS, WIDTH), lambda i: (0, 0, 0)),
        ],
        out_shape=[
            jax.ShapeDtypeStruct((ROWS, 2 * WIDTH), BF16),
            jax.ShapeDtypeStruct((ROWS, WIDTH), BF16),
            jax.ShapeDtypeStruct((4, PART_ROWS, WIDTH), BF16),
        ],
        compiler_params=pltpu.CompilerParams(vmem_limit_bytes=VMEM_LIMIT),
        name="first_panel",
    )(assembled, inverses, child)


def piece_of(z):
    return jnp.where(z < 4, z ^ 1, z - 4)


def product_kernel(
    where_ref, front_ref, inverse_ref, first_ref, firsts_ref, nexts_ref, column_ref, mine_ref, beside_ref, across_ref,
    zero_ref, one_ref, two_ref, three_ref, factor_ref, second_ref, weight_ref, rows_ref, columns_ref, held_ref, sem,
):
    copy = pltpu.make_async_copy(column_ref, held_ref, sem)
    copy.start()
    r, z = where_ref[0], where_ref[1]
    other = jnp.where(z % 2 == 1, (z + 1) % 8, (z + 7) % 8)
    here, there = piece_of(z), piece_of(other)

    def put(piece, value):
        second_ref[pl.ds(pl.multiple_of(piece * ROWS, ROWS), ROWS), :] = value

    put(here, mine_ref[...])
    put(here ^ 1, beside_ref[...])
    put(there, across_ref[:ROWS])
    put(there ^ 1, across_ref[ROWS:])
    inverse = inverse_ref[0, 0]

    turned = lax.dot_general(
        second_ref[...], inverse, (((0,), (0,)), ((), ())), preferred_element_type=F32
    )
    high = turned.astype(BF16)
    weight_ref[0] = high
    weight_ref[1] = (turned - high.astype(F32)).astype(BF16)

    def panel_of(first, following):
        lost = dot(first, weight_ref[0]) + dot(first, weight_ref[1])
        return dot(following, inverse) - lost

    own = front_ref[0] - dot_t(first_ref[...], second_ref[...])
    own = dot_split(own, inverse, 3)
    own = jnp.where((r == 0) & (z < 4), jnp.zeros_like(own), own)
    factor_ref[0, :, :WIDTH] = first_ref[...]
    factor_ref[0, :, WIDTH:] = own.astype(BF16)

    first = firsts_ref[...].reshape(4 * ROWS, WIDTH)
    panel = panel_of(first, nexts_ref[...].reshape(4 * ROWS, WIDTH))
    above = lax.broadcasted_iota(jnp.int32, (4 * ROWS, WIDTH), 0) < jnp.where(z < 4, ROWS, 0)
    panel = jnp.where(above, jnp.zeros_like(panel), panel).astype(BF16)
    for k in range(4):
        place = pl.ds(pl.multiple_of(((k - r + 4) % 4) * ROWS, ROWS), ROWS)
        rows_ref[place, :WIDTH] = first[k * ROWS : (k + 1) * ROWS]
        rows_ref[place, WIDTH:] = panel[k * ROWS : (k + 1) * ROWS]
    copy.wait()
    for half in range(2):
        place = pl.ds(half * 4 * ROWS, 4 * ROWS)
        first = held_ref[4 * half : 4 * half + 4].reshape(4 * ROWS, 2 * WIDTH)
        columns_ref[place, :WIDTH] = first[:, :WIDTH]
        columns_ref[place, WIDTH:] = panel_of(first[:, :WIDTH], first[:, WIDTH:]).astype(BF16)
    for part in range(4):
        place = pl.ds(part * 256, 256)
        total = dot_t(rows_ref[...], columns_ref[place, :]).astype(BF16)
        for k, ref in enumerate((zero_ref, one_ref, two_ref, three_ref)):
            ref[:, place] = total[k * ROWS : (k + 1) * ROWS]


def products(where, assembled, inverses, first, firsts, nexts, columns, mine, beside, across):
    whole = lambda *shape: pl.BlockSpec(shape, lambda i, w: (0,) * len(shape))
    return pl.pallas_call(
        product_kernel,
        grid_spec=pltpu.PrefetchScalarGridSpec(
            num_scalar_prefetch=1,
            grid=(1,),
            in_specs=[
                pl.BlockSpec((1, ROWS, WIDTH), lambda i, w: (0, 0, 1)),
                pl.BlockSpec((1, 1, WIDTH, WIDTH), lambda i, w: (0, 1, 0, 0)),
                whole(ROWS, WIDTH),
                whole(4, ROWS, WIDTH),
                whole(4, ROWS, WIDTH),
                pl.BlockSpec(memory_space=pl.ANY),
                whole(ROWS, WIDTH),
                whole(ROWS, WIDTH),
                whole(2 * ROWS, WIDTH),
            ],
            out_specs=[whole(ROWS, GROUP)] * 4 + [whole(1, ROWS, 2 * WIDTH)],
            scratch_shapes=[
                pltpu.VMEM((WIDTH, WIDTH), BF16),
                pltpu.VMEM((2, WIDTH, WIDTH), BF16),
                pltpu.VMEM((4 * ROWS, 2 * WIDTH), BF16),
                pltpu.VMEM((8 * ROWS, 2 * WIDTH), BF16),
                pltpu.VMEM((8, ROWS, 2 * WIDTH), BF16),
                pltpu.SemaphoreType.DMA,
            ],
        ),
        out_shape=[jax.ShapeDtypeStruct((ROWS, GROUP), BF16)] * 4
        + [jax.ShapeDtypeStruct((1, ROWS, 2 * WIDTH), BF16)],
        compiler_params=pltpu.CompilerParams(vmem_limit_bytes=VMEM_LIMIT),
        name="products",
    )(where, assembled, inverses, first, firsts, nexts, columns, mine, beside, across)


PIECES = (
    ((0, 0, 48, 0), (1, 0, 48, 48), (2, 0, 32, 96)),
    ((2, 32, 16, 0), (3, 0, 48, 16), (4, 0, 48, 64), (5, 0, 16, 112)),
    ((5, 16, 32, 0), (6, 0, 48, 32), (7, 0, 48, 80)),
)


def final_kernel(
    where_ref, front_ref, zero_ref, one_ref, two_ref, three_ref, child_ref, schur_ref, block_ref, sems
):
    step = pl.program_id(0)
    r, z = where_ref[0], where_ref[1]
    target = r * 8 + z
    found, child = jnp.int32(0), jnp.int32(0)
    for b in range(CHILD_BLOCKS):
        hit = (where_ref[2 + b] == target).astype(jnp.int32)
        found, child = found + hit, child + hit * b
    turn = child % 3

    def copies(j):
        return [
            pltpu.make_async_copy(
                child_ref.at[z_from, pl.ds(start, rows), :],
                block_ref.at[pl.ds(place, rows), :],
                sems.at[i],
            )
            for i, (z_from, start, rows, place) in enumerate(PIECES[j])
        ]

    for j in range(3):
        @pl.when((step == 0) & (found > 0) & (turn == j))
        def _():
            for copy in copies(j):
                copy.start()

    for k, ref in enumerate((zero_ref, one_ref, two_ref, three_ref)):
        @pl.when((r - step + 3) % 4 == k)
        def _():
            schur_ref[0] = front_ref[0] - ref[...].astype(F32)

    for j in range(3):
        @pl.when((step == 1) & (found > 0) & (turn == j))
        def _():
            for copy in copies(j):
                copy.wait()

    for b in range(CHILD_BLOCKS):
        parent = where_ref[2 + b]
        @pl.when((found > 0) & (step > 0) & (parent // 8 == step + 1))
        def _():
            place = pl.ds(pl.multiple_of((parent % 8) * ROWS, ROWS), ROWS)
            schur_ref[0, :, place] += block_ref[:, b * ROWS : (b + 1) * ROWS].astype(F32)


def final(where, assembled, pieces, children):
    return pl.pallas_call(
        final_kernel,
        grid_spec=pltpu.PrefetchScalarGridSpec(
            num_scalar_prefetch=1,
            grid=(3,),
            in_specs=[pl.BlockSpec((1, ROWS, GROUP), lambda i, w: (0, 0, i + 1))]
            + [pl.BlockSpec((ROWS, GROUP), lambda i, w: (0, 0))] * 4
            + [pl.BlockSpec(memory_space=pl.ANY)],
            out_specs=pl.BlockSpec((1, ROWS, GROUP), lambda i, w: (0, 0, i)),
            scratch_shapes=[
                pltpu.VMEM((ROWS, CHILD), BF16),
                pltpu.SemaphoreType.DMA((4,)),
            ],
        ),
        out_shape=jax.ShapeDtypeStruct((1, ROWS, 3 * GROUP), F32),
        compiler_params=pltpu.CompilerParams(vmem_limit_bytes=VMEM_LIMIT),
        name="final",
    )(where, assembled, *pieces, children)


def wanted_kernel(where_ref, parts_ref, out_ref):
    r = where_ref[0]
    for z in range(8):
        child = jnp.int32(0)
        for b in range(CHILD_BLOCKS):
            child = child + jnp.where(where_ref[2 + b] == r * 8 + z, b, 0)
        for part in range(3):
            start = ROWS + part * CHILD_ROWS
            piece = parts_ref[child // 3, start : start + CHILD_ROWS]
            out_ref[z, :, part * WIDTH : (part + 1) * WIDTH] = piece


def wanted(where, parts):
    whole = lambda *shape: pl.BlockSpec(shape, lambda i, w: (0,) * len(shape))
    return pl.pallas_call(
        wanted_kernel,
        grid_spec=pltpu.PrefetchScalarGridSpec(
            num_scalar_prefetch=1,
            grid=(1,),
            in_specs=[whole(4, PART_ROWS, WIDTH)],
            out_specs=whole(8, CHILD_ROWS, CHILD),
        ),
        out_shape=jax.ShapeDtypeStruct((8, CHILD_ROWS, CHILD), BF16),
        compiler_params=pltpu.CompilerParams(vmem_limit_bytes=VMEM_LIMIT),
        name="wanted",
    )(where, parts)


def on_device(assembled, update, blocks, inverses):
    r, z = lax.axis_index("row"), lax.axis_index("col")
    where = jnp.concatenate([jnp.stack([r, z]).astype(jnp.int32), blocks[0]])

    child = lax.ppermute(update[0], "front", [(i, i ^ 1) for i in range(16)])
    both, first, parts = first_panel(assembled, inverses, child)
    columns = lax.all_gather(both, "col", axis=0)
    firsts = lax.all_gather(first, "row", axis=0)

    top = firsts[0]
    parts, top = lax.optimization_barrier((parts, top))
    parts = lax.all_to_all(parts, "row", 0, 0)
    passed = lax.ppermute(top, "col", [(4, 1), (5, 0), (6, 3), (7, 2)])
    mine = jnp.where(z < 4, passed, top)
    beside = lax.ppermute(mine, "col", [(i, i ^ 1) for i in range(8)])
    across = lax.ppermute(
        jnp.concatenate([mine, beside]),
        "col",
        [(i, (i + 1) % 8 if i % 2 else (i + 7) % 8) for i in range(8)],
    )
    pieces = wanted(where, parts)
    across, pieces = lax.optimization_barrier((across, pieces))
    children = lax.all_to_all(pieces, "col", 0, 0)

    *pieces, factor = products(
        where, assembled, inverses, first, firsts, parts, columns, mine, beside, across
    )
    for s in range(1, 4):
        pairs = [(i, (i + s) % 4) for i in range(1, 4)]
        pieces[s] = lax.ppermute(pieces[s], "row", pairs)
    return factor, final(where, assembled, pieces, children)


def solution(mesh):
    return jax.shard_map(
        on_device,
        mesh=mesh,
        in_specs=(
            P("front", ("row", "col"), None),
            P("front", ("row", "col"), None),
            P("front", None),
            P("front", None, None, None),
        ),
        out_specs=(P("front", ("row", "col"), None), P("front", ("row", "col"), None)),
        check_vma=False,
    )
```

```python
import jax
import jax.numpy as jnp
from jax import lax
from jax.experimental import pallas as pl
from jax.experimental.pallas import tpu as pltpu
from jax.sharding import PartitionSpec as P

WIDTH = 512
ROWS = 128
GROUP = 1024
CHILD = 1536
CHILD_BLOCKS = 12
CHILD_ROWS = 48
PART_ROWS = ROWS + 3 * CHILD_ROWS
VMEM_LIMIT = 60 * 1024 * 1024

F32 = jnp.float32
BF16 = jnp.bfloat16


def dot(a, b):
    return jnp.dot(a, b, preferred_element_type=F32)


def dot_t(a, b):
    return lax.dot_general(a, b, (((1,), (1,)), ((), ())), preferred_element_type=F32)


def dot_split(a, b, terms):
    total = None
    for _ in range(terms):
        part = a.astype(BF16)
        a = a - part.astype(F32)
        product = dot(part, b)
        total = product if total is None else total + product
    return total


def first_kernel(front_ref, inverse_ref, both_ref, first_ref):
    first = dot_split(front_ref[0, :, :WIDTH], inverse_ref[0, 0], 3).astype(BF16)
    both_ref[:, :WIDTH] = first
    both_ref[:, WIDTH:] = front_ref[0, :, WIDTH:].astype(BF16)
    first_ref[...] = first


def first_panel(assembled, inverses):
    return pl.pallas_call(
        first_kernel,
        grid=(1,),
        in_specs=[
            pl.BlockSpec((1, ROWS, 2 * WIDTH), lambda i: (0, 0, 0)),
            pl.BlockSpec((1, 1, WIDTH, WIDTH), lambda i: (0, 0, 0, 0)),
        ],
        out_specs=[
            pl.BlockSpec((ROWS, 2 * WIDTH), lambda i: (0, 0)),
            pl.BlockSpec((ROWS, WIDTH), lambda i: (0, 0)),
        ],
        out_shape=[
            jax.ShapeDtypeStruct((ROWS, 2 * WIDTH), BF16),
            jax.ShapeDtypeStruct((ROWS, WIDTH), BF16),
        ],
        compiler_params=pltpu.CompilerParams(vmem_limit_bytes=VMEM_LIMIT),
        name="first_panel",
    )(assembled, inverses)


def pack_kernel(both_ref, child_ref, parts_ref):
    for k in range(4):
        parts_ref[k, :ROWS] = both_ref[...]
        for part in range(3):
            start = ROWS + part * CHILD_ROWS
            parts_ref[k, start : start + CHILD_ROWS] = child_ref[:, part * WIDTH : (part + 1) * WIDTH]


def pack(both, child):
    return pl.pallas_call(
        pack_kernel,
        grid=(1,),
        in_specs=[
            pl.BlockSpec((ROWS, WIDTH), lambda i: (0, 1)),
            pl.BlockSpec((CHILD_ROWS, CHILD), lambda i: (0, 0)),
        ],
        out_specs=pl.BlockSpec((4, PART_ROWS, WIDTH), lambda i: (0, 0, 0)),
        out_shape=jax.ShapeDtypeStruct((4, PART_ROWS, WIDTH), BF16),
        compiler_params=pltpu.CompilerParams(vmem_limit_bytes=VMEM_LIMIT),
        name="pack",
    )(both, child)


def piece_of(z):
    return jnp.where(z < 4, z ^ 1, z - 4)


def put_second(z, second_ref, mine_ref, beside_ref, across_ref):
    here, there = piece_of(z), piece_of((z + 2 * (z % 2) + 7) % 8)
    pieces = (
        (here, mine_ref[...]),
        (here ^ 1, beside_ref[...]),
        (there, across_ref[:ROWS]),
        (there ^ 1, across_ref[ROWS:]),
    )
    for piece, value in pieces:
        second_ref[pl.ds(pl.multiple_of(piece * ROWS, ROWS), ROWS), :] = value


def factor_kernel(
    where_ref, front_ref, inverse_ref, first_ref, mine_ref, beside_ref, across_ref, factor_ref, second_ref
):
    r, z = where_ref[0], where_ref[1]
    put_second(z, second_ref, mine_ref, beside_ref, across_ref)
    own = front_ref[0] - dot_t(first_ref[...], second_ref[...])
    own = dot_split(own, inverse_ref[0, 0], 3)
    own = jnp.where((r == 0) & (z < 4), jnp.zeros_like(own), own)
    factor_ref[0, :, :WIDTH] = first_ref[...]
    factor_ref[0, :, WIDTH:] = own.astype(BF16)


def own_factor(where, assembled, inverses, first, relay):
    whole = lambda *shape: pl.BlockSpec(shape, lambda i, w: (0,) * len(shape))
    return pl.pallas_call(
        factor_kernel,
        grid_spec=pltpu.PrefetchScalarGridSpec(
            num_scalar_prefetch=1,
            grid=(1,),
            in_specs=[
                pl.BlockSpec((1, ROWS, WIDTH), lambda i, w: (0, 0, 1)),
                pl.BlockSpec((1, 1, WIDTH, WIDTH), lambda i, w: (0, 1, 0, 0)),
                whole(ROWS, WIDTH),
                whole(ROWS, WIDTH),
                whole(ROWS, WIDTH),
                whole(2 * ROWS, WIDTH),
            ],
            out_specs=whole(1, ROWS, 2 * WIDTH),
            scratch_shapes=[pltpu.VMEM((WIDTH, WIDTH), BF16)],
        ),
        out_shape=jax.ShapeDtypeStruct((1, ROWS, 2 * WIDTH), BF16),
        compiler_params=pltpu.CompilerParams(vmem_limit_bytes=VMEM_LIMIT),
        cost_estimate=pl.CostEstimate(flops=2**28, bytes_accessed=2**21, transcendentals=0),
        name="own_factor",
    )(where, assembled, inverses, first, *relay)


def product_kernel(
    where_ref, inverse_ref, firsts_ref, nexts_ref, column_ref, mine_ref, beside_ref, across_ref,
    zero_ref, one_ref, two_ref, three_ref, second_ref, weight_ref, rows_ref, columns_ref, held_ref, sem,
):
    copy = pltpu.make_async_copy(column_ref, held_ref, sem)
    copy.start()
    r, z = where_ref[0], where_ref[1]
    put_second(z, second_ref, mine_ref, beside_ref, across_ref)
    inverse = inverse_ref[0, 0]

    turned = lax.dot_general(
        second_ref[...], inverse, (((0,), (0,)), ((), ())), preferred_element_type=F32
    )
    high = turned.astype(BF16)
    weight_ref[0] = high
    weight_ref[1] = (turned - high.astype(F32)).astype(BF16)

    def panel_of(first, following):
        lost = dot(first, weight_ref[0]) + dot(first, weight_ref[1])
        return dot(following, inverse) - lost

    first = firsts_ref[...].reshape(4 * ROWS, WIDTH)
    panel = panel_of(first, nexts_ref[...].reshape(4 * ROWS, WIDTH))
    above = lax.broadcasted_iota(jnp.int32, (4 * ROWS, WIDTH), 0) < jnp.where(z < 4, ROWS, 0)
    panel = jnp.where(above, jnp.zeros_like(panel), panel).astype(BF16)
    for k in range(4):
        place = pl.ds(pl.multiple_of(((k - r + 4) % 4) * ROWS, ROWS), ROWS)
        rows_ref[place, :WIDTH] = first[k * ROWS : (k + 1) * ROWS]
        rows_ref[place, WIDTH:] = panel[k * ROWS : (k + 1) * ROWS]
    copy.wait()
    for half in range(2):
        place = pl.ds(half * 4 * ROWS, 4 * ROWS)
        first = held_ref[4 * half : 4 * half + 4].reshape(4 * ROWS, 2 * WIDTH)
        columns_ref[place, :WIDTH] = first[:, :WIDTH]
        columns_ref[place, WIDTH:] = panel_of(first[:, :WIDTH], first[:, WIDTH:]).astype(BF16)
    for part in range(4):
        place = pl.ds(part * 256, 256)
        total = dot_t(rows_ref[...], columns_ref[place, :]).astype(BF16)
        for k, ref in enumerate((zero_ref, one_ref, two_ref, three_ref)):
            ref[:, place] = total[k * ROWS : (k + 1) * ROWS]


def products(where, inverses, firsts, nexts, columns, relay):
    whole = lambda *shape: pl.BlockSpec(shape, lambda i, w: (0,) * len(shape))
    return pl.pallas_call(
        product_kernel,
        grid_spec=pltpu.PrefetchScalarGridSpec(
            num_scalar_prefetch=1,
            grid=(1,),
            in_specs=[
                pl.BlockSpec((1, 1, WIDTH, WIDTH), lambda i, w: (0, 1, 0, 0)),
                whole(4, ROWS, WIDTH),
                whole(4, ROWS, WIDTH),
                pl.BlockSpec(memory_space=pl.ANY),
                whole(ROWS, WIDTH),
                whole(ROWS, WIDTH),
                whole(2 * ROWS, WIDTH),
            ],
            out_specs=[whole(ROWS, GROUP)] * 4,
            scratch_shapes=[
                pltpu.VMEM((WIDTH, WIDTH), BF16),
                pltpu.VMEM((2, WIDTH, WIDTH), BF16),
                pltpu.VMEM((4 * ROWS, 2 * WIDTH), BF16),
                pltpu.VMEM((8 * ROWS, 2 * WIDTH), BF16),
                pltpu.VMEM((8, ROWS, 2 * WIDTH), BF16),
                pltpu.SemaphoreType.DMA,
            ],
        ),
        out_shape=[jax.ShapeDtypeStruct((ROWS, GROUP), BF16)] * 4,
        compiler_params=pltpu.CompilerParams(vmem_limit_bytes=VMEM_LIMIT),
        name="products",
    )(where, inverses, firsts, nexts, columns, *relay)


PIECES = (
    ((0, 0, 48, 0), (1, 0, 48, 48), (2, 0, 32, 96)),
    ((2, 32, 16, 0), (3, 0, 48, 16), (4, 0, 48, 64), (5, 0, 16, 112)),
    ((5, 16, 32, 0), (6, 0, 48, 32), (7, 0, 48, 80)),
)


def final_kernel(
    where_ref, front_ref, zero_ref, one_ref, two_ref, three_ref, child_ref, schur_ref,
    held_ref, product_ref, block_ref, read_sems, child_sems, write_sems,
):
    r, z = where_ref[0], where_ref[1]
    target = r * 8 + z
    found, child = jnp.int32(0), jnp.int32(0)
    for b in range(CHILD_BLOCKS):
        hit = (where_ref[2 + b] == target).astype(jnp.int32)
        found, child = found + hit, child + hit * b
    turn = child % 3

    def read_front(g):
        place = pl.ds((g + 1) * GROUP, GROUP)
        return pltpu.make_async_copy(front_ref.at[0, :, place], held_ref.at[g], read_sems.at[0, g])

    def read_product(g, ref):
        return pltpu.make_async_copy(ref, product_ref.at[g], read_sems.at[1, g])

    def write(g):
        place = pl.ds(g * GROUP, GROUP)
        return pltpu.make_async_copy(held_ref.at[g], schur_ref.at[0, :, place], write_sems.at[g])

    def read_child(j):
        return [
            pltpu.make_async_copy(
                child_ref.at[z_from, pl.ds(part * CHILD_ROWS + start, rows), :],
                block_ref.at[pl.ds(place, rows), pl.ds(part * WIDTH, WIDTH)],
                child_sems.at[i, part],
            )
            for i, (z_from, start, rows, place) in enumerate(PIECES[j])
            for part in range(3)
        ]

    for g in range(3):
        read_front(g).start()
        for k, ref in enumerate((zero_ref, one_ref, two_ref, three_ref)):
            @pl.when((r - g + 3) % 4 == k)
            def _():
                read_product(g, ref).start()
    for j in range(3):
        @pl.when((found > 0) & (turn == j))
        def _():
            for copy in read_child(j):
                copy.start()

    for g in range(3):
        read_front(g).wait()
        read_product(g, zero_ref).wait()
        held_ref[g] = held_ref[g] - product_ref[g].astype(F32)
        if g == 1:
            for j in range(3):
                @pl.when((found > 0) & (turn == j))
                def _():
                    for copy in read_child(j):
                        copy.wait()
        if g >= 1:
            for b in range(CHILD_BLOCKS):
                parent = where_ref[2 + b]
                @pl.when((found > 0) & (parent // 8 == g + 1))
                def _():
                    place = pl.ds(pl.multiple_of((parent % 8) * ROWS, ROWS), ROWS)
                    held_ref[g, :, place] += block_ref[:, b * ROWS : (b + 1) * ROWS].astype(F32)
        write(g).start()
    for g in range(3):
        write(g).wait()


def final(where, assembled, pieces, children):
    return pl.pallas_call(
        final_kernel,
        grid_spec=pltpu.PrefetchScalarGridSpec(
            num_scalar_prefetch=1,
            grid=(1,),
            in_specs=[pl.BlockSpec(memory_space=pl.ANY)] * 6,
            out_specs=pl.BlockSpec(memory_space=pl.ANY),
            scratch_shapes=[
                pltpu.VMEM((3, ROWS, GROUP), F32),
                pltpu.VMEM((3, ROWS, GROUP), BF16),
                pltpu.VMEM((ROWS, CHILD), BF16),
                pltpu.SemaphoreType.DMA((2, 3)),
                pltpu.SemaphoreType.DMA((4, 3)),
                pltpu.SemaphoreType.DMA((3,)),
            ],
        ),
        out_shape=jax.ShapeDtypeStruct((1, ROWS, 3 * GROUP), F32),
        compiler_params=pltpu.CompilerParams(vmem_limit_bytes=VMEM_LIMIT),
        name="final",
    )(where, assembled, *pieces, children)


def wanted_kernel(where_ref, parts_ref, out_ref, sems):
    r = where_ref[0]
    copies = []
    for z in range(8):
        child = jnp.int32(0)
        for b in range(CHILD_BLOCKS):
            child = child + jnp.where(where_ref[2 + b] == r * 8 + z, b, 0)
        source = parts_ref.at[jnp.minimum(child // 3, 3), pl.ds(ROWS, 3 * CHILD_ROWS), :]
        copies.append(pltpu.make_async_copy(source, out_ref.at[z], sems.at[z]))
        copies[z].start()
    for copy in copies:
        copy.wait()


def wanted(where, parts):
    return pl.pallas_call(
        wanted_kernel,
        grid_spec=pltpu.PrefetchScalarGridSpec(
            num_scalar_prefetch=1,
            grid=(1,),
            in_specs=[pl.BlockSpec((4, PART_ROWS, WIDTH), lambda i, w: (0, 0, 0))],
            out_specs=pl.BlockSpec(memory_space=pl.ANY),
            scratch_shapes=[pltpu.SemaphoreType.DMA((8,))],
        ),
        out_shape=jax.ShapeDtypeStruct((8, 3 * CHILD_ROWS, WIDTH), BF16),
        compiler_params=pltpu.CompilerParams(vmem_limit_bytes=VMEM_LIMIT),
        name="wanted",
    )(where, parts)


def on_device(assembled, update, blocks, inverses):
    r, z = lax.axis_index("row"), lax.axis_index("col")
    where = jnp.concatenate([jnp.stack([r, z]).astype(jnp.int32), blocks[0]])

    both, first = first_panel(assembled, inverses)
    columns = lax.all_gather(both, "col", axis=0)
    first, update = lax.optimization_barrier((first, update))
    child = lax.ppermute(update[0], "front", [(i, i ^ 1) for i in range(16)])
    firsts = lax.all_gather(first, "row", axis=0)

    top = firsts[0]
    child, top = lax.optimization_barrier((child, top))
    parts = lax.all_to_all(pack(both, child), "row", 0, 0)
    passed = lax.ppermute(top, "col", [(4, 1), (5, 0), (6, 3), (7, 2)])
    mine = jnp.where(z < 4, passed, top)
    beside = lax.ppermute(mine, "col", [(i, i ^ 1) for i in range(8)])
    across = lax.ppermute(
        jnp.concatenate([mine, beside]),
        "col",
        [(i, (i + 1) % 8 if i % 2 else (i + 7) % 8) for i in range(8)],
    )
    relay = mine, beside, across
    pieces = wanted(where, parts)
    relay, pieces = lax.optimization_barrier((relay, pieces))
    children = lax.all_to_all(pieces, "col", 0, 0)

    pieces = list(products(where, inverses, firsts, parts, columns, relay))
    factor = own_factor(where, assembled, inverses, first, relay)
    for s in range(1, 4):
        pairs = [(i, (i + s) % 4) for i in range(1, 4)]
        pieces[s] = lax.ppermute(pieces[s], "row", pairs)
    return factor, final(where, assembled, pieces, children)


def solution(mesh):
    return jax.shard_map(
        on_device,
        mesh=mesh,
        in_specs=(
            P("front", ("row", "col"), None),
            P("front", ("row", "col"), None),
            P("front", None),
            P("front", None, None, None),
        ),
        out_specs=(P("front", ("row", "col"), None), P("front", ("row", "col"), None)),
        check_vma=False,
    )
```

```python
import jax
import jax.numpy as jnp
from jax import lax
from jax.experimental import pallas as pl
from jax.experimental.pallas import tpu as pltpu
from jax.sharding import PartitionSpec as P

WIDTH = 512
ROWS = 128
GROUP = 1024
CHILD = 1536
CHILD_BLOCKS = 12
CHILD_ROWS = 48
PART_ROWS = ROWS + 3 * CHILD_ROWS
MIB = 1024 * 1024
VMEM_LIMIT = 60 * MIB

F32 = jnp.float32
BF16 = jnp.bfloat16


def dot(a, b):
    return jnp.dot(a, b, preferred_element_type=F32)


def dot_t(a, b):
    return lax.dot_general(a, b, (((1,), (1,)), ((), ())), preferred_element_type=F32)


def dot_split(a, b, terms):
    total = None
    for _ in range(terms):
        part = a.astype(BF16)
        a = a - part.astype(F32)
        product = dot(part, b)
        total = product if total is None else total + product
    return total


def first_kernel(front_ref, inverse_ref, both_ref, first_ref):
    first = dot_split(front_ref[0, :, :WIDTH], inverse_ref[0, 0], 3).astype(BF16)
    both_ref[:, :WIDTH] = first
    both_ref[:, WIDTH:] = front_ref[0, :, WIDTH:].astype(BF16)
    first_ref[...] = first


def first_panel(assembled, inverses):
    return pl.pallas_call(
        first_kernel,
        grid=(1,),
        in_specs=[
            pl.BlockSpec((1, ROWS, 2 * WIDTH), lambda i: (0, 0, 0)),
            pl.BlockSpec((1, 1, WIDTH, WIDTH), lambda i: (0, 0, 0, 0)),
        ],
        out_specs=[
            pl.BlockSpec((ROWS, 2 * WIDTH), lambda i: (0, 0)),
            pl.BlockSpec((ROWS, WIDTH), lambda i: (0, 0)),
        ],
        out_shape=[
            jax.ShapeDtypeStruct((ROWS, 2 * WIDTH), BF16),
            jax.ShapeDtypeStruct((ROWS, WIDTH), BF16),
        ],
        compiler_params=pltpu.CompilerParams(vmem_limit_bytes=VMEM_LIMIT),
        name="first_panel",
    )(assembled, inverses)


def pack_kernel(both_ref, child_ref, parts_ref):
    for k in range(4):
        parts_ref[k, :ROWS] = both_ref[...]
        for part in range(3):
            start = ROWS + part * CHILD_ROWS
            parts_ref[k, start : start + CHILD_ROWS] = child_ref[:, part * WIDTH : (part + 1) * WIDTH]


def pack(both, child):
    return pl.pallas_call(
        pack_kernel,
        grid=(1,),
        in_specs=[
            pl.BlockSpec((ROWS, WIDTH), lambda i: (0, 1)),
            pl.BlockSpec((CHILD_ROWS, CHILD), lambda i: (0, 0)),
        ],
        out_specs=pl.BlockSpec((4, PART_ROWS, WIDTH), lambda i: (0, 0, 0)),
        out_shape=jax.ShapeDtypeStruct((4, PART_ROWS, WIDTH), BF16),
        compiler_params=pltpu.CompilerParams(vmem_limit_bytes=8 * MIB),
        name="pack",
    )(both, child)


def piece_of(z):
    return jnp.where(z < 4, z ^ 1, z - 4)


def mine_kernel(where_ref, passed_ref, top_ref, mine_ref):
    mine_ref[...] = jnp.where(where_ref[1] < 4, passed_ref[...], top_ref[0])


def first_relay(where, passed, firsts):
    return pl.pallas_call(
        mine_kernel,
        grid_spec=pltpu.PrefetchScalarGridSpec(
            num_scalar_prefetch=1,
            grid=(1,),
            in_specs=[
                pl.BlockSpec((ROWS, WIDTH), lambda i, w: (0, 0)),
                pl.BlockSpec((1, ROWS, WIDTH), lambda i, w: (0, 0, 0)),
            ],
            out_specs=pl.BlockSpec((ROWS, WIDTH), lambda i, w: (0, 0)),
        ),
        out_shape=jax.ShapeDtypeStruct((ROWS, WIDTH), BF16),
        compiler_params=pltpu.CompilerParams(vmem_limit_bytes=8 * MIB),
        cost_estimate=pl.CostEstimate(flops=11_800_000_000, bytes_accessed=2**20, transcendentals=0),
        name="first_relay",
    )(where, passed, firsts)


def put_second(z, second_ref, mine_ref, beside_ref, across_ref):
    here, there = piece_of(z), piece_of((z + 2 * (z % 2) + 7) % 8)
    pieces = (
        (here, mine_ref[...]),
        (here ^ 1, beside_ref[...]),
        (there, across_ref[:ROWS]),
        (there ^ 1, across_ref[ROWS:]),
    )
    for piece, value in pieces:
        second_ref[pl.ds(pl.multiple_of(piece * ROWS, ROWS), ROWS), :] = value


def factor_kernel(
    where_ref, front_ref, inverse_ref, first_ref, mine_ref, beside_ref, across_ref, factor_ref, second_ref
):
    r, z = where_ref[0], where_ref[1]
    put_second(z, second_ref, mine_ref, beside_ref, across_ref)
    own = front_ref[0] - dot_t(first_ref[...], second_ref[...])
    own = dot_split(own, inverse_ref[0, 0], 3)
    own = jnp.where((r == 0) & (z < 4), jnp.zeros_like(own), own)
    factor_ref[0, :, :WIDTH] = first_ref[...]
    factor_ref[0, :, WIDTH:] = own.astype(BF16)


def own_factor(where, assembled, inverses, first, relay):
    whole = lambda *shape: pl.BlockSpec(shape, lambda i, w: (0,) * len(shape))
    return pl.pallas_call(
        factor_kernel,
        grid_spec=pltpu.PrefetchScalarGridSpec(
            num_scalar_prefetch=1,
            grid=(1,),
            in_specs=[
                pl.BlockSpec((1, ROWS, WIDTH), lambda i, w: (0, 0, 1)),
                pl.BlockSpec((1, 1, WIDTH, WIDTH), lambda i, w: (0, 1, 0, 0)),
                whole(ROWS, WIDTH),
                whole(ROWS, WIDTH),
                whole(ROWS, WIDTH),
                whole(2 * ROWS, WIDTH),
            ],
            out_specs=whole(1, ROWS, 2 * WIDTH),
            scratch_shapes=[pltpu.VMEM((WIDTH, WIDTH), BF16)],
        ),
        out_shape=jax.ShapeDtypeStruct((1, ROWS, 2 * WIDTH), BF16),
        compiler_params=pltpu.CompilerParams(vmem_limit_bytes=8 * MIB),
        cost_estimate=pl.CostEstimate(flops=2**28, bytes_accessed=2**21, transcendentals=0),
        name="own_factor",
    )(where, assembled, inverses, first, *relay)


def product_kernel(
    where_ref, inverse_ref, firsts_ref, nexts_ref, column_ref, mine_ref, beside_ref, across_ref,
    zero_ref, one_ref, two_ref, three_ref, second_ref, weight_ref, rows_ref, columns_ref, held_ref, sem,
):
    copy = pltpu.make_async_copy(column_ref, held_ref, sem)
    copy.start()
    r, z = where_ref[0], where_ref[1]
    put_second(z, second_ref, mine_ref, beside_ref, across_ref)
    inverse = inverse_ref[0, 0]

    turned = lax.dot_general(
        second_ref[...], inverse, (((0,), (0,)), ((), ())), preferred_element_type=F32
    )
    high = turned.astype(BF16)
    weight_ref[0] = high
    weight_ref[1] = (turned - high.astype(F32)).astype(BF16)

    def panel_of(first, following):
        lost = dot(first, weight_ref[0]) + dot(first, weight_ref[1])
        return dot(following, inverse) - lost

    first = firsts_ref[...].reshape(4 * ROWS, WIDTH)
    panel = panel_of(first, nexts_ref[...].reshape(4 * ROWS, WIDTH))
    above = lax.broadcasted_iota(jnp.int32, (4 * ROWS, WIDTH), 0) < jnp.where(z < 4, ROWS, 0)
    panel = jnp.where(above, jnp.zeros_like(panel), panel).astype(BF16)
    for k in range(4):
        place = pl.ds(pl.multiple_of(((k - r + 4) % 4) * ROWS, ROWS), ROWS)
        rows_ref[place, :WIDTH] = first[k * ROWS : (k + 1) * ROWS]
        rows_ref[place, WIDTH:] = panel[k * ROWS : (k + 1) * ROWS]
    copy.wait()
    for half in range(2):
        place = pl.ds(half * 4 * ROWS, 4 * ROWS)
        first = held_ref[4 * half : 4 * half + 4].reshape(4 * ROWS, 2 * WIDTH)
        columns_ref[place, :WIDTH] = first[:, :WIDTH]
        columns_ref[place, WIDTH:] = panel_of(first[:, :WIDTH], first[:, WIDTH:]).astype(BF16)
    for part in range(4):
        place = pl.ds(part * 256, 256)
        total = dot_t(rows_ref[...], columns_ref[place, :]).astype(BF16)
        for k, ref in enumerate((zero_ref, one_ref, two_ref, three_ref)):
            ref[:, place] = total[k * ROWS : (k + 1) * ROWS]


def products(where, inverses, firsts, nexts, columns, relay):
    whole = lambda *shape: pl.BlockSpec(shape, lambda i, w: (0,) * len(shape))
    return pl.pallas_call(
        product_kernel,
        grid_spec=pltpu.PrefetchScalarGridSpec(
            num_scalar_prefetch=1,
            grid=(1,),
            in_specs=[
                pl.BlockSpec((1, 1, WIDTH, WIDTH), lambda i, w: (0, 1, 0, 0)),
                whole(4, ROWS, WIDTH),
                whole(4, ROWS, WIDTH),
                pl.BlockSpec(memory_space=pl.ANY),
                whole(ROWS, WIDTH),
                whole(ROWS, WIDTH),
                whole(2 * ROWS, WIDTH),
            ],
            out_specs=[whole(ROWS, GROUP)] * 4,
            scratch_shapes=[
                pltpu.VMEM((WIDTH, WIDTH), BF16),
                pltpu.VMEM((2, WIDTH, WIDTH), BF16),
                pltpu.VMEM((4 * ROWS, 2 * WIDTH), BF16),
                pltpu.VMEM((8 * ROWS, 2 * WIDTH), BF16),
                pltpu.VMEM((8, ROWS, 2 * WIDTH), BF16),
                pltpu.SemaphoreType.DMA,
            ],
        ),
        out_shape=[jax.ShapeDtypeStruct((ROWS, GROUP), BF16)] * 4,
        compiler_params=pltpu.CompilerParams(vmem_limit_bytes=58 * MIB),
        name="products",
    )(where, inverses, firsts, nexts, columns, *relay)


PIECES = (
    ((0, 0, 48, 0), (1, 0, 48, 48), (2, 0, 32, 96)),
    ((2, 32, 16, 0), (3, 0, 48, 16), (4, 0, 48, 64), (5, 0, 16, 112)),
    ((5, 16, 32, 0), (6, 0, 48, 32), (7, 0, 48, 80)),
)


def final_kernel(
    where_ref, front_ref, zero_ref, one_ref, two_ref, three_ref, child_ref, schur_ref,
    held_ref, product_ref, block_ref, read_sems, child_sems, write_sems,
):
    r, z = where_ref[0], where_ref[1]
    target = r * 8 + z
    found, child = jnp.int32(0), jnp.int32(0)
    for b in range(CHILD_BLOCKS):
        hit = (where_ref[2 + b] == target).astype(jnp.int32)
        found, child = found + hit, child + hit * b
    turn = child % 3

    def read_front(g):
        place = pl.ds((g + 1) * GROUP, GROUP)
        return pltpu.make_async_copy(front_ref.at[0, :, place], held_ref.at[g], read_sems.at[0, g])

    def read_product(g, ref):
        return pltpu.make_async_copy(ref, product_ref.at[g], read_sems.at[1, g])

    def write(g):
        place = pl.ds(g * GROUP, GROUP)
        return pltpu.make_async_copy(held_ref.at[g], schur_ref.at[0, :, place], write_sems.at[g])

    def read_child(j):
        return [
            pltpu.make_async_copy(
                child_ref.at[z_from, pl.ds(part * CHILD_ROWS + start, rows), :],
                block_ref.at[pl.ds(place, rows), pl.ds(part * WIDTH, WIDTH)],
                child_sems.at[i, part],
            )
            for i, (z_from, start, rows, place) in enumerate(PIECES[j])
            for part in range(3)
        ]

    for g in range(3):
        read_front(g).start()
        for k, ref in enumerate((zero_ref, one_ref, two_ref, three_ref)):
            @pl.when((r - g + 3) % 4 == k)
            def _():
                read_product(g, ref).start()
    for j in range(3):
        @pl.when((found > 0) & (turn == j))
        def _():
            for copy in read_child(j):
                copy.start()

    for g in range(3):
        read_front(g).wait()
        read_product(g, zero_ref).wait()
        held_ref[g] = held_ref[g] - product_ref[g].astype(F32)
        if g == 1:
            for j in range(3):
                @pl.when((found > 0) & (turn == j))
                def _():
                    for copy in read_child(j):
                        copy.wait()
        if g >= 1:
            for b in range(CHILD_BLOCKS):
                parent = where_ref[2 + b]
                @pl.when((found > 0) & (parent // 8 == g + 1))
                def _():
                    place = pl.ds(pl.multiple_of((parent % 8) * ROWS, ROWS), ROWS)
                    held_ref[g, :, place] += block_ref[:, b * ROWS : (b + 1) * ROWS].astype(F32)
        write(g).start()
    for g in range(3):
        write(g).wait()


def final(where, assembled, pieces, children):
    return pl.pallas_call(
        final_kernel,
        grid_spec=pltpu.PrefetchScalarGridSpec(
            num_scalar_prefetch=1,
            grid=(1,),
            in_specs=[pl.BlockSpec(memory_space=pl.ANY)] * 6,
            out_specs=pl.BlockSpec(memory_space=pl.ANY),
            scratch_shapes=[
                pltpu.VMEM((3, ROWS, GROUP), F32),
                pltpu.VMEM((3, ROWS, GROUP), BF16),
                pltpu.VMEM((ROWS, CHILD), BF16),
                pltpu.SemaphoreType.DMA((2, 3)),
                pltpu.SemaphoreType.DMA((4, 3)),
                pltpu.SemaphoreType.DMA((3,)),
            ],
        ),
        out_shape=jax.ShapeDtypeStruct((1, ROWS, 3 * GROUP), F32),
        compiler_params=pltpu.CompilerParams(vmem_limit_bytes=8 * MIB),
        name="final",
    )(where, assembled, *pieces, children)


def wanted_kernel(where_ref, parts_ref, out_ref, sems):
    r = where_ref[0]
    copies = []
    for z in range(8):
        child = jnp.int32(0)
        for b in range(CHILD_BLOCKS):
            child = child + jnp.where(where_ref[2 + b] == r * 8 + z, b, 0)
        source = parts_ref.at[jnp.minimum(child // 3, 3), pl.ds(ROWS, 3 * CHILD_ROWS), :]
        copies.append(pltpu.make_async_copy(source, out_ref.at[z], sems.at[z]))
        copies[z].start()
    for copy in copies:
        copy.wait()


def wanted(where, parts):
    return pl.pallas_call(
        wanted_kernel,
        grid_spec=pltpu.PrefetchScalarGridSpec(
            num_scalar_prefetch=1,
            grid=(1,),
            in_specs=[pl.BlockSpec((4, PART_ROWS, WIDTH), lambda i, w: (0, 0, 0))],
            out_specs=pl.BlockSpec(memory_space=pl.ANY),
            scratch_shapes=[pltpu.SemaphoreType.DMA((8,))],
        ),
        out_shape=jax.ShapeDtypeStruct((8, 3 * CHILD_ROWS, WIDTH), BF16),
        compiler_params=pltpu.CompilerParams(vmem_limit_bytes=8 * MIB),
        name="wanted",
    )(where, parts)


def on_device(assembled, update, blocks, inverses):
    r, z = lax.axis_index("row"), lax.axis_index("col")
    where = jnp.concatenate([jnp.stack([r, z]).astype(jnp.int32), blocks[0]])

    both, first = first_panel(assembled, inverses)
    columns = lax.all_gather(both, "col", axis=0)
    first, update = lax.optimization_barrier((first, update))
    child = lax.ppermute(update[0], "front", [(i, i ^ 1) for i in range(16)])
    firsts = lax.all_gather(first, "row", axis=0)

    top = firsts[0]
    child, top = lax.optimization_barrier((child, top))
    parts = lax.all_to_all(pack(both, child), "row", 0, 0)
    passed = lax.ppermute(top, "col", [(4, 1), (5, 0), (6, 3), (7, 2)])
    mine = first_relay(where, passed, firsts)
    beside = lax.ppermute(mine, "col", [(i, i ^ 1) for i in range(8)])
    across = lax.ppermute(
        jnp.concatenate([mine, beside]),
        "col",
        [(i, (i + 1) % 8 if i % 2 else (i + 7) % 8) for i in range(8)],
    )
    relay = mine, beside, across
    pieces = wanted(where, parts)
    relay, pieces = lax.optimization_barrier((relay, pieces))
    children = lax.all_to_all(pieces, "col", 0, 0)

    pieces = list(products(where, inverses, firsts, parts, columns, relay))
    factor = own_factor(where, assembled, inverses, first, relay)
    for s in range(1, 4):
        pairs = [(i, (i + s) % 4) for i in range(1, 4)]
        pieces[s] = lax.ppermute(pieces[s], "row", pairs)
    return factor, final(where, assembled, pieces, children)


def solution(mesh):
    return jax.shard_map(
        on_device,
        mesh=mesh,
        in_specs=(
            P("front", ("row", "col"), None),
            P("front", ("row", "col"), None),
            P("front", None),
            P("front", None, None, None),
        ),
        out_specs=(P("front", ("row", "col"), None), P("front", ("row", "col"), None)),
        check_vma=False,
    )
```

```python
import jax
import jax.numpy as jnp
from jax import lax
from jax.experimental import pallas as pl
from jax.experimental.pallas import tpu as pltpu
from jax.sharding import PartitionSpec as P

WIDTH = 512
ROWS = 128
GROUP = 1024
SENT = GROUP - ROWS
CHILD = 1536
CHILD_BLOCKS = 12
CHILD_ROWS = 48
PART_ROWS = ROWS + 3 * CHILD_ROWS
MIB = 1024 * 1024
VMEM_LIMIT = 60 * MIB

F32 = jnp.float32
BF16 = jnp.bfloat16


def dot(a, b):
    return jnp.dot(a, b, preferred_element_type=F32)


def dot_t(a, b):
    return lax.dot_general(a, b, (((1,), (1,)), ((), ())), preferred_element_type=F32)


def dot_split(a, b, terms):
    total = None
    for _ in range(terms):
        part = a.astype(BF16)
        a = a - part.astype(F32)
        product = dot(part, b)
        total = product if total is None else total + product
    return total


def first_kernel(front_ref, inverse_ref, both_ref, first_ref):
    first = dot_split(front_ref[0, :, :WIDTH], inverse_ref[0, 0], 3).astype(BF16)
    both_ref[:, :WIDTH] = first
    both_ref[:, WIDTH:] = front_ref[0, :, WIDTH:].astype(BF16)
    first_ref[...] = first


def first_panel(assembled, inverses):
    return pl.pallas_call(
        first_kernel,
        grid=(1,),
        in_specs=[
            pl.BlockSpec((1, ROWS, 2 * WIDTH), lambda i: (0, 0, 0)),
            pl.BlockSpec((1, 1, WIDTH, WIDTH), lambda i: (0, 0, 0, 0)),
        ],
        out_specs=[
            pl.BlockSpec((ROWS, 2 * WIDTH), lambda i: (0, 0)),
            pl.BlockSpec((ROWS, WIDTH), lambda i: (0, 0)),
        ],
        out_shape=[
            jax.ShapeDtypeStruct((ROWS, 2 * WIDTH), BF16),
            jax.ShapeDtypeStruct((ROWS, WIDTH), BF16),
        ],
        compiler_params=pltpu.CompilerParams(vmem_limit_bytes=VMEM_LIMIT),
        name="first_panel",
    )(assembled, inverses)


def pack_kernel(both_ref, child_ref, parts_ref):
    for k in range(4):
        parts_ref[k, :ROWS] = both_ref[...]
        for part in range(3):
            start = ROWS + part * CHILD_ROWS
            parts_ref[k, start : start + CHILD_ROWS] = child_ref[:, part * WIDTH : (part + 1) * WIDTH]


def pack(both, child):
    return pl.pallas_call(
        pack_kernel,
        grid=(1,),
        in_specs=[
            pl.BlockSpec((ROWS, WIDTH), lambda i: (0, 1)),
            pl.BlockSpec((CHILD_ROWS, CHILD), lambda i: (0, 0)),
        ],
        out_specs=pl.BlockSpec((4, PART_ROWS, WIDTH), lambda i: (0, 0, 0)),
        out_shape=jax.ShapeDtypeStruct((4, PART_ROWS, WIDTH), BF16),
        compiler_params=pltpu.CompilerParams(vmem_limit_bytes=8 * MIB),
        name="pack",
    )(both, child)


def piece_of(z):
    return jnp.where(z < 4, z ^ 1, z - 4)


def mine_kernel(where_ref, passed_ref, top_ref, mine_ref):
    mine_ref[...] = jnp.where(where_ref[1] < 4, passed_ref[...], top_ref[0])


def first_relay(where, passed, firsts):
    return pl.pallas_call(
        mine_kernel,
        grid_spec=pltpu.PrefetchScalarGridSpec(
            num_scalar_prefetch=1,
            grid=(1,),
            in_specs=[
                pl.BlockSpec((ROWS, WIDTH), lambda i, w: (0, 0)),
                pl.BlockSpec((1, ROWS, WIDTH), lambda i, w: (0, 0, 0)),
            ],
            out_specs=pl.BlockSpec((ROWS, WIDTH), lambda i, w: (0, 0)),
        ),
        out_shape=jax.ShapeDtypeStruct((ROWS, WIDTH), BF16),
        compiler_params=pltpu.CompilerParams(vmem_limit_bytes=8 * MIB),
        cost_estimate=pl.CostEstimate(flops=11_800_000_000, bytes_accessed=2**20, transcendentals=0),
        name="first_relay",
    )(where, passed, firsts)


def put_second(z, second_ref, mine_ref, beside_ref, across_ref):
    here, there = piece_of(z), piece_of((z + 2 * (z % 2) + 7) % 8)
    pieces = (
        (here, mine_ref[...]),
        (here ^ 1, beside_ref[...]),
        (there, across_ref[:ROWS]),
        (there ^ 1, across_ref[ROWS:]),
    )
    for piece, value in pieces:
        second_ref[pl.ds(pl.multiple_of(piece * ROWS, ROWS), ROWS), :] = value


def factor_kernel(
    where_ref, front_ref, inverse_ref, first_ref, mine_ref, beside_ref, across_ref, factor_ref, second_ref
):
    r, z = where_ref[0], where_ref[1]
    put_second(z, second_ref, mine_ref, beside_ref, across_ref)
    own = front_ref[0] - dot_t(first_ref[...], second_ref[...])
    own = dot_split(own, inverse_ref[0, 0], 3)
    own = jnp.where((r == 0) & (z < 4), jnp.zeros_like(own), own)
    factor_ref[0, :, :WIDTH] = first_ref[...]
    factor_ref[0, :, WIDTH:] = own.astype(BF16)


def own_factor(where, assembled, inverses, first, relay):
    whole = lambda *shape: pl.BlockSpec(shape, lambda i, w: (0,) * len(shape))
    return pl.pallas_call(
        factor_kernel,
        grid_spec=pltpu.PrefetchScalarGridSpec(
            num_scalar_prefetch=1,
            grid=(1,),
            in_specs=[
                pl.BlockSpec((1, ROWS, WIDTH), lambda i, w: (0, 0, 1)),
                pl.BlockSpec((1, 1, WIDTH, WIDTH), lambda i, w: (0, 1, 0, 0)),
                whole(ROWS, WIDTH),
                whole(ROWS, WIDTH),
                whole(ROWS, WIDTH),
                whole(2 * ROWS, WIDTH),
            ],
            out_specs=whole(1, ROWS, 2 * WIDTH),
            scratch_shapes=[pltpu.VMEM((WIDTH, WIDTH), BF16)],
        ),
        out_shape=jax.ShapeDtypeStruct((1, ROWS, 2 * WIDTH), BF16),
        compiler_params=pltpu.CompilerParams(vmem_limit_bytes=8 * MIB),
        cost_estimate=pl.CostEstimate(flops=2**28, bytes_accessed=2**21, transcendentals=0),
        name="own_factor",
    )(where, assembled, inverses, first, *relay)


def product_kernel(
    where_ref, inverse_ref, firsts_ref, nexts_ref, column_ref, mine_ref, beside_ref, across_ref,
    zero_ref, one_ref, two_ref, three_ref, across_groups_ref,
    held_inverse_ref, second_ref, weight_ref, rows_ref, next_ref, columns_ref, following_ref, sems,
):
    r, z = where_ref[0], where_ref[1]

    def rows_at(place):
        return pl.ds(pl.multiple_of(place * ROWS, ROWS), ROWS)

    def await_all(ref, sem):
        pltpu.make_async_copy(ref, ref, sem).wait()

    here, there = piece_of(z), piece_of((z + 2 * (z % 2) + 7) % 8)
    pieces = (
        (here, mine_ref),
        (here ^ 1, beside_ref),
        (there, across_ref.at[:ROWS]),
        (there ^ 1, across_ref.at[ROWS:]),
    )
    for place, ref in pieces:
        pltpu.make_async_copy(ref, second_ref.at[rows_at(place)], sems.at[0]).start()
    pltpu.make_async_copy(inverse_ref.at[0, 1], held_inverse_ref, sems.at[1]).start()
    for k in range(4):
        place = rows_at((k - r + 4) % 4)
        part = rows_ref.at[place, pl.ds(0, WIDTH)]
        pltpu.make_async_copy(firsts_ref.at[k], part, sems.at[2]).start()
        part = nexts_ref.at[k, pl.ds(0, ROWS)]
        pltpu.make_async_copy(part, next_ref.at[place], sems.at[3]).start()
    for j in range(8):
        place = rows_at((j - z + 7) % 8)
        part = column_ref.at[j, :, pl.ds(0, WIDTH)]
        pltpu.make_async_copy(part, columns_ref.at[place, pl.ds(0, WIDTH)], sems.at[4]).start()
        part = column_ref.at[j, :, pl.ds(WIDTH, WIDTH)]
        pltpu.make_async_copy(part, following_ref.at[place], sems.at[5]).start()

    await_all(second_ref, sems.at[0])
    await_all(held_inverse_ref, sems.at[1])
    inverse = held_inverse_ref[...]
    turned = lax.dot_general(
        second_ref[...], inverse, (((0,), (0,)), ((), ())), preferred_element_type=F32
    )
    high = turned.astype(BF16)
    weight_ref[0] = high
    weight_ref[1] = (turned - high.astype(F32)).astype(BF16)

    def panel_of(first, following):
        lost = dot(first, weight_ref[0]) + dot(first, weight_ref[1])
        return dot(following, inverse) - lost

    await_all(rows_ref.at[:, pl.ds(0, WIDTH)], sems.at[2])
    await_all(next_ref, sems.at[3])
    panel = panel_of(rows_ref[:, :WIDTH], next_ref[...])
    top = jnp.where(z < 4, (4 - r) % 4, 4)
    above = lax.broadcasted_iota(jnp.int32, (4 * ROWS, WIDTH), 0) // ROWS == top
    rows_ref[:, WIDTH:] = jnp.where(above, jnp.zeros_like(panel), panel).astype(BF16)
    await_all(columns_ref.at[:, pl.ds(0, WIDTH)], sems.at[4])
    await_all(following_ref, sems.at[5])
    for half in range(2):
        place = pl.ds(half * 4 * ROWS, 4 * ROWS)
        panel = panel_of(columns_ref[place, :WIDTH], following_ref[place, :])
        columns_ref[place, WIDTH:] = panel.astype(BF16)
    for part in range(4):
        place = pl.ds(part * 256, 256)
        total = dot_t(rows_ref[...], columns_ref[place, :]).astype(BF16)
        zero_ref[:, place] = total[:ROWS]
        width = min(256, SENT - part * 256)
        for k, ref in enumerate((one_ref, two_ref, three_ref), 1):
            ref[:, part * 256 : part * 256 + width] = total[k * ROWS : (k + 1) * ROWS, :width]
    across_groups_ref[...] = dot_t(rows_ref[:ROWS, :], rows_ref[...]).astype(BF16)


def products(where, inverses, firsts, nexts, columns, relay):
    whole = lambda *shape: pl.BlockSpec(shape, lambda i, w: (0,) * len(shape))
    widths = GROUP, SENT, SENT, SENT, 4 * ROWS
    return pl.pallas_call(
        product_kernel,
        grid_spec=pltpu.PrefetchScalarGridSpec(
            num_scalar_prefetch=1,
            grid=(1,),
            in_specs=[pl.BlockSpec(memory_space=pl.ANY)] * 7,
            out_specs=[whole(ROWS, width) for width in widths],
            scratch_shapes=[
                pltpu.VMEM((WIDTH, WIDTH), BF16),
                pltpu.VMEM((WIDTH, WIDTH), BF16),
                pltpu.VMEM((2, WIDTH, WIDTH), BF16),
                pltpu.VMEM((4 * ROWS, 2 * WIDTH), BF16),
                pltpu.VMEM((4 * ROWS, WIDTH), BF16),
                pltpu.VMEM((8 * ROWS, 2 * WIDTH), BF16),
                pltpu.VMEM((8 * ROWS, WIDTH), BF16),
                pltpu.SemaphoreType.DMA((6,)),
            ],
        ),
        out_shape=[jax.ShapeDtypeStruct((ROWS, width), BF16) for width in widths],
        compiler_params=pltpu.CompilerParams(vmem_limit_bytes=58 * MIB),
        name="products",
    )(where, inverses, firsts, nexts, columns, *relay)


PIECES = (
    ((0, 0, 48, 0), (1, 0, 48, 48), (2, 0, 32, 96)),
    ((2, 32, 16, 0), (3, 0, 48, 16), (4, 0, 48, 64), (5, 0, 16, 112)),
    ((5, 16, 32, 0), (6, 0, 48, 32), (7, 0, 48, 80)),
)


def final_kernel(
    where_ref, front_ref, zero_ref, one_ref, two_ref, three_ref, across_groups_ref, child_ref, schur_ref,
    held_ref, product_ref, block_ref, read_sems, child_sems, write_sems,
):
    r, z = where_ref[0], where_ref[1]
    target = r * 8 + z
    found, child = jnp.int32(0), jnp.int32(0)
    for b in range(CHILD_BLOCKS):
        hit = (where_ref[2 + b] == target).astype(jnp.int32)
        found, child = found + hit, child + hit * b
    turn = child % 3

    def read_front(g):
        place = pl.ds((g + 1) * GROUP, GROUP)
        return pltpu.make_async_copy(front_ref.at[0, :, place], held_ref.at[g], read_sems.at[0, g])

    def read_product(g, k):
        if k == 0:
            return [pltpu.make_async_copy(zero_ref, product_ref.at[g], read_sems.at[1, g])]
        sent = product_ref.at[g, :, pl.ds(0, SENT)]
        kept = product_ref.at[g, :, pl.ds(SENT, ROWS)]
        place = pl.ds((4 - k) * ROWS, ROWS)
        return [
            pltpu.make_async_copy((one_ref, two_ref, three_ref)[k - 1], sent, read_sems.at[1, g]),
            pltpu.make_async_copy(across_groups_ref.at[:, place], kept, read_sems.at[1, g]),
        ]

    def write(g):
        place = pl.ds(g * GROUP, GROUP)
        return pltpu.make_async_copy(held_ref.at[g], schur_ref.at[0, :, place], write_sems.at[g])

    def read_child(j):
        return [
            pltpu.make_async_copy(
                child_ref.at[z_from, pl.ds(part * CHILD_ROWS + start, rows), :],
                block_ref.at[pl.ds(place, rows), pl.ds(part * WIDTH, WIDTH)],
                child_sems.at[i, part],
            )
            for i, (z_from, start, rows, place) in enumerate(PIECES[j])
            for part in range(3)
        ]

    for g in range(3):
        read_front(g).start()
        for k in range(4):
            @pl.when((r - g + 3) % 4 == k)
            def _():
                for copy in read_product(g, k):
                    copy.start()
    for j in range(3):
        @pl.when((found > 0) & (turn == j))
        def _():
            for copy in read_child(j):
                copy.start()

    for g in range(3):
        read_front(g).wait()
        read_product(g, 0)[0].wait()
        for i in range(8):
            place = pl.ds(pl.multiple_of((z + 1 + i) % 8 * ROWS, ROWS), ROWS)
            held_ref[g, :, place] -= product_ref[g, :, i * ROWS : (i + 1) * ROWS].astype(F32)
        if g == 1:
            for j in range(3):
                @pl.when((found > 0) & (turn == j))
                def _():
                    for copy in read_child(j):
                        copy.wait()
        if g >= 1:
            for b in range(CHILD_BLOCKS):
                parent = where_ref[2 + b]
                @pl.when((found > 0) & (parent // 8 == g + 1))
                def _():
                    place = pl.ds(pl.multiple_of((parent % 8) * ROWS, ROWS), ROWS)
                    held_ref[g, :, place] += block_ref[:, b * ROWS : (b + 1) * ROWS].astype(F32)
        write(g).start()
    for g in range(3):
        write(g).wait()


def final(where, assembled, pieces, children):
    return pl.pallas_call(
        final_kernel,
        grid_spec=pltpu.PrefetchScalarGridSpec(
            num_scalar_prefetch=1,
            grid=(1,),
            in_specs=[pl.BlockSpec(memory_space=pl.ANY)] * 7,
            out_specs=pl.BlockSpec(memory_space=pl.ANY),
            scratch_shapes=[
                pltpu.VMEM((3, ROWS, GROUP), F32),
                pltpu.VMEM((3, ROWS, GROUP), BF16),
                pltpu.VMEM((ROWS, CHILD), BF16),
                pltpu.SemaphoreType.DMA((2, 3)),
                pltpu.SemaphoreType.DMA((4, 3)),
                pltpu.SemaphoreType.DMA((3,)),
            ],
        ),
        out_shape=jax.ShapeDtypeStruct((1, ROWS, 3 * GROUP), F32),
        compiler_params=pltpu.CompilerParams(vmem_limit_bytes=8 * MIB),
        name="final",
    )(where, assembled, *pieces, children)


def wanted_kernel(where_ref, parts_ref, out_ref, sems):
    r = where_ref[0]
    copies = []
    for z in range(8):
        child = jnp.int32(0)
        for b in range(CHILD_BLOCKS):
            child = child + jnp.where(where_ref[2 + b] == r * 8 + z, b, 0)
        source = parts_ref.at[jnp.minimum(child // 3, 3), pl.ds(ROWS, 3 * CHILD_ROWS), :]
        copies.append(pltpu.make_async_copy(source, out_ref.at[z], sems.at[z]))
        copies[z].start()
    for copy in copies:
        copy.wait()


def wanted(where, parts):
    return pl.pallas_call(
        wanted_kernel,
        grid_spec=pltpu.PrefetchScalarGridSpec(
            num_scalar_prefetch=1,
            grid=(1,),
            in_specs=[pl.BlockSpec((4, PART_ROWS, WIDTH), lambda i, w: (0, 0, 0))],
            out_specs=pl.BlockSpec(memory_space=pl.ANY),
            scratch_shapes=[pltpu.SemaphoreType.DMA((8,))],
        ),
        out_shape=jax.ShapeDtypeStruct((8, 3 * CHILD_ROWS, WIDTH), BF16),
        compiler_params=pltpu.CompilerParams(vmem_limit_bytes=8 * MIB),
        name="wanted",
    )(where, parts)


def on_device(assembled, update, blocks, inverses):
    r, z = lax.axis_index("row"), lax.axis_index("col")
    where = jnp.concatenate([jnp.stack([r, z]).astype(jnp.int32), blocks[0]])

    both, first = first_panel(assembled, inverses)
    columns = lax.all_gather(both, "col", axis=0)
    first, update = lax.optimization_barrier((first, update))
    child = lax.ppermute(update[0], "front", [(i, i ^ 1) for i in range(16)])
    firsts = lax.all_gather(first, "row", axis=0)

    top = firsts[0]
    child, top = lax.optimization_barrier((child, top))
    parts = lax.all_to_all(pack(both, child), "row", 0, 0)
    passed = lax.ppermute(top, "col", [(4, 1), (5, 0), (6, 3), (7, 2)])
    mine = first_relay(where, passed, firsts)
    beside = lax.ppermute(mine, "col", [(i, i ^ 1) for i in range(8)])
    across = lax.ppermute(
        jnp.concatenate([mine, beside]),
        "col",
        [(i, (i + 1) % 8 if i % 2 else (i + 7) % 8) for i in range(8)],
    )
    relay = mine, beside, across
    pieces = wanted(where, parts)
    relay, pieces = lax.optimization_barrier((relay, pieces))
    children = lax.all_to_all(pieces, "col", 0, 0)

    zero, one, two, three, across_groups = products(where, inverses, firsts, parts, columns, relay)
    factor = own_factor(where, assembled, inverses, first, relay)
    two = lax.ppermute(two, "row", [(i, (i + 2) % 4) for i in range(1, 4)])
    one = lax.ppermute(one, "row", [(i, (i + 1) % 4) for i in range(1, 4)])
    three = lax.ppermute(three, "row", [(i, (i + 3) % 4) for i in range(1, 4)])
    pieces = zero, one, two, three, across_groups
    return factor, final(where, assembled, pieces, children)


def solution(mesh):
    return jax.shard_map(
        on_device,
        mesh=mesh,
        in_specs=(
            P("front", ("row", "col"), None),
            P("front", ("row", "col"), None),
            P("front", None),
            P("front", None, None, None),
        ),
        out_specs=(P("front", ("row", "col"), None), P("front", ("row", "col"), None)),
        check_vma=False,
    )
```

```python
import jax
import jax.numpy as jnp
from jax import lax
from jax.experimental import pallas as pl
from jax.experimental.pallas import tpu as pltpu
from jax.sharding import PartitionSpec as P

WIDTH = 512
ROWS = 128
GROUP = 1024
SENT = GROUP - ROWS
CHILD = 1536
CHILD_BLOCKS = 12
CHILD_ROWS = 48
HALF = CHILD // 2
THIRD = 256
PART_ROWS = 2 * ROWS + 3 * CHILD_ROWS
MIB = 1024 * 1024
VMEM_LIMIT = 60 * MIB

F32 = jnp.float32
BF16 = jnp.bfloat16


def dot(a, b):
    return jnp.dot(a, b, preferred_element_type=F32)


def dot_t(a, b):
    return lax.dot_general(a, b, (((1,), (1,)), ((), ())), preferred_element_type=F32)


def dot_split(a, b, terms):
    total = None
    for _ in range(terms):
        part = a.astype(BF16)
        a = a - part.astype(F32)
        product = dot(part, b)
        total = product if total is None else total + product
    return total


def first_kernel(front_ref, inverse_ref, both_ref, first_ref):
    first = dot_split(front_ref[0, :, :WIDTH], inverse_ref[0, 0], 3).astype(BF16)
    both_ref[:, :WIDTH] = first
    both_ref[:, WIDTH:] = front_ref[0, :, WIDTH:].astype(BF16)
    first_ref[...] = first


def first_panel(assembled, inverses):
    return pl.pallas_call(
        first_kernel,
        grid=(1,),
        in_specs=[
            pl.BlockSpec((1, ROWS, 2 * WIDTH), lambda i: (0, 0, 0)),
            pl.BlockSpec((1, 1, WIDTH, WIDTH), lambda i: (0, 0, 0, 0)),
        ],
        out_specs=[
            pl.BlockSpec((ROWS, 2 * WIDTH), lambda i: (0, 0)),
            pl.BlockSpec((ROWS, WIDTH), lambda i: (0, 0)),
        ],
        out_shape=[
            jax.ShapeDtypeStruct((ROWS, 2 * WIDTH), BF16),
            jax.ShapeDtypeStruct((ROWS, WIDTH), BF16),
        ],
        compiler_params=pltpu.CompilerParams(vmem_limit_bytes=VMEM_LIMIT),
        name="first_panel",
    )(assembled, inverses)


def pack_kernel(both_ref, child_ref, parts_ref):
    for k in range(4):
        for half in range(2):
            place = slice(half * ROWS, (half + 1) * ROWS)
            parts_ref[k, place] = both_ref[:, half * THIRD : (half + 1) * THIRD]
        first = 0 if k >= 2 else HALF
        for part in range(3):
            start = 2 * ROWS + part * CHILD_ROWS
            column = first + part * THIRD
            parts_ref[k, start : start + CHILD_ROWS] = child_ref[:, column : column + THIRD]


def pack(both, child):
    return pl.pallas_call(
        pack_kernel,
        grid=(1,),
        in_specs=[
            pl.BlockSpec((ROWS, WIDTH), lambda i: (0, 1)),
            pl.BlockSpec((CHILD_ROWS, CHILD), lambda i: (0, 0)),
        ],
        out_specs=pl.BlockSpec((4, PART_ROWS, THIRD), lambda i: (0, 0, 0)),
        out_shape=jax.ShapeDtypeStruct((4, PART_ROWS, THIRD), BF16),
        compiler_params=pltpu.CompilerParams(vmem_limit_bytes=8 * MIB),
        name="pack",
    )(both, child)


def piece_of(z):
    return jnp.where(z < 4, z ^ 1, z - 4)


def mine_kernel(where_ref, passed_ref, top_ref, mine_ref):
    mine_ref[...] = jnp.where(where_ref[1] < 4, passed_ref[...], top_ref[0])


def first_relay(where, passed, firsts):
    return pl.pallas_call(
        mine_kernel,
        grid_spec=pltpu.PrefetchScalarGridSpec(
            num_scalar_prefetch=1,
            grid=(1,),
            in_specs=[
                pl.BlockSpec((ROWS, WIDTH), lambda i, w: (0, 0)),
                pl.BlockSpec((1, ROWS, WIDTH), lambda i, w: (0, 0, 0)),
            ],
            out_specs=pl.BlockSpec((ROWS, WIDTH), lambda i, w: (0, 0)),
        ),
        out_shape=jax.ShapeDtypeStruct((ROWS, WIDTH), BF16),
        compiler_params=pltpu.CompilerParams(vmem_limit_bytes=8 * MIB),
        cost_estimate=pl.CostEstimate(flops=11_800_000_000, bytes_accessed=2**20, transcendentals=0),
        name="first_relay",
    )(where, passed, firsts)


def put_second(z, second_ref, mine_ref, beside_ref, across_ref):
    here, there = piece_of(z), piece_of((z + 2 * (z % 2) + 7) % 8)
    pieces = (
        (here, mine_ref[...]),
        (here ^ 1, beside_ref[...]),
        (there, across_ref[:ROWS]),
        (there ^ 1, across_ref[ROWS:]),
    )
    for piece, value in pieces:
        second_ref[pl.ds(pl.multiple_of(piece * ROWS, ROWS), ROWS), :] = value


def factor_kernel(
    where_ref, front_ref, inverse_ref, first_ref, mine_ref, beside_ref, across_ref, factor_ref, second_ref
):
    r, z = where_ref[0], where_ref[1]
    put_second(z, second_ref, mine_ref, beside_ref, across_ref)
    own = front_ref[0] - dot_t(first_ref[...], second_ref[...])
    own = dot_split(own, inverse_ref[0, 0], 3)
    own = jnp.where((r == 0) & (z < 4), jnp.zeros_like(own), own)
    factor_ref[0, :, :WIDTH] = first_ref[...]
    factor_ref[0, :, WIDTH:] = own.astype(BF16)


def own_factor(where, assembled, inverses, first, relay):
    whole = lambda *shape: pl.BlockSpec(shape, lambda i, w: (0,) * len(shape))
    return pl.pallas_call(
        factor_kernel,
        grid_spec=pltpu.PrefetchScalarGridSpec(
            num_scalar_prefetch=1,
            grid=(1,),
            in_specs=[
                pl.BlockSpec((1, ROWS, WIDTH), lambda i, w: (0, 0, 1)),
                pl.BlockSpec((1, 1, WIDTH, WIDTH), lambda i, w: (0, 1, 0, 0)),
                whole(ROWS, WIDTH),
                whole(ROWS, WIDTH),
                whole(ROWS, WIDTH),
                whole(2 * ROWS, WIDTH),
            ],
            out_specs=whole(1, ROWS, 2 * WIDTH),
            scratch_shapes=[pltpu.VMEM((WIDTH, WIDTH), BF16)],
        ),
        out_shape=jax.ShapeDtypeStruct((1, ROWS, 2 * WIDTH), BF16),
        compiler_params=pltpu.CompilerParams(vmem_limit_bytes=8 * MIB),
        cost_estimate=pl.CostEstimate(flops=2**28, bytes_accessed=2**21, transcendentals=0),
        name="own_factor",
    )(where, assembled, inverses, first, *relay)


def product_kernel(
    where_ref, inverse_ref, firsts_ref, nexts_ref, column_ref, mine_ref, beside_ref, across_ref,
    zero_ref, one_ref, two_ref, three_ref, across_groups_ref,
    held_inverse_ref, second_ref, weight_ref, rows_ref, next_ref, columns_ref, following_ref, sems,
):
    r, z = where_ref[0], where_ref[1]

    def rows_at(place):
        return pl.ds(pl.multiple_of(place * ROWS, ROWS), ROWS)

    def await_all(ref, sem):
        pltpu.make_async_copy(ref, ref, sem).wait()

    here, there = piece_of(z), piece_of((z + 2 * (z % 2) + 7) % 8)
    pieces = (
        (here, mine_ref),
        (here ^ 1, beside_ref),
        (there, across_ref.at[:ROWS]),
        (there ^ 1, across_ref.at[ROWS:]),
    )
    for place, ref in pieces:
        pltpu.make_async_copy(ref, second_ref.at[rows_at(place)], sems.at[0]).start()
    pltpu.make_async_copy(inverse_ref.at[0, 1], held_inverse_ref, sems.at[1]).start()
    for k in range(4):
        place = rows_at((k - r + 4) % 4)
        part = rows_ref.at[place, pl.ds(0, WIDTH)]
        pltpu.make_async_copy(firsts_ref.at[k], part, sems.at[2]).start()
        for half in range(2):
            source = nexts_ref.at[k, pl.ds(half * ROWS, ROWS), :]
            part = next_ref.at[place, pl.ds(half * THIRD, THIRD)]
            pltpu.make_async_copy(source, part, sems.at[3]).start()
    for j in range(8):
        place = rows_at((j - z + 7) % 8)
        part = column_ref.at[j, :, pl.ds(0, WIDTH)]
        pltpu.make_async_copy(part, columns_ref.at[place, pl.ds(0, WIDTH)], sems.at[4]).start()
        part = column_ref.at[j, :, pl.ds(WIDTH, WIDTH)]
        pltpu.make_async_copy(part, following_ref.at[place], sems.at[5]).start()

    await_all(second_ref, sems.at[0])
    await_all(held_inverse_ref, sems.at[1])
    inverse = held_inverse_ref[...]
    turned = lax.dot_general(
        second_ref[...], inverse, (((0,), (0,)), ((), ())), preferred_element_type=F32
    )
    high = turned.astype(BF16)
    weight_ref[0] = high
    weight_ref[1] = (turned - high.astype(F32)).astype(BF16)

    def panel_of(first, following):
        lost = dot(first, weight_ref[0]) + dot(first, weight_ref[1])
        return dot(following, inverse) - lost

    await_all(rows_ref.at[:, pl.ds(0, WIDTH)], sems.at[2])
    await_all(next_ref, sems.at[3])
    panel = panel_of(rows_ref[:, :WIDTH], next_ref[...])
    top = jnp.where(z < 4, (4 - r) % 4, 4)
    above = lax.broadcasted_iota(jnp.int32, (4 * ROWS, WIDTH), 0) // ROWS == top
    rows_ref[:, WIDTH:] = jnp.where(above, jnp.zeros_like(panel), panel).astype(BF16)
    await_all(columns_ref.at[:, pl.ds(0, WIDTH)], sems.at[4])
    await_all(following_ref, sems.at[5])
    for half in range(2):
        place = pl.ds(half * 4 * ROWS, 4 * ROWS)
        panel = panel_of(columns_ref[place, :WIDTH], following_ref[place, :])
        columns_ref[place, WIDTH:] = panel.astype(BF16)
    for part in range(4):
        place = pl.ds(part * 256, 256)
        total = dot_t(rows_ref[...], columns_ref[place, :]).astype(BF16)
        zero_ref[:, place] = total[:ROWS]
        width = min(256, SENT - part * 256)
        for k, ref in enumerate((one_ref, two_ref, three_ref), 1):
            ref[:, part * 256 : part * 256 + width] = total[k * ROWS : (k + 1) * ROWS, :width]
    across_groups_ref[...] = dot_t(rows_ref[:ROWS, :], rows_ref[...]).astype(BF16)


def products(where, inverses, firsts, nexts, columns, relay):
    whole = lambda *shape: pl.BlockSpec(shape, lambda i, w: (0,) * len(shape))
    widths = GROUP, SENT, SENT, SENT, 4 * ROWS
    return pl.pallas_call(
        product_kernel,
        grid_spec=pltpu.PrefetchScalarGridSpec(
            num_scalar_prefetch=1,
            grid=(1,),
            in_specs=[pl.BlockSpec(memory_space=pl.ANY)] * 7,
            out_specs=[whole(ROWS, width) for width in widths],
            scratch_shapes=[
                pltpu.VMEM((WIDTH, WIDTH), BF16),
                pltpu.VMEM((WIDTH, WIDTH), BF16),
                pltpu.VMEM((2, WIDTH, WIDTH), BF16),
                pltpu.VMEM((4 * ROWS, 2 * WIDTH), BF16),
                pltpu.VMEM((4 * ROWS, WIDTH), BF16),
                pltpu.VMEM((8 * ROWS, 2 * WIDTH), BF16),
                pltpu.VMEM((8 * ROWS, WIDTH), BF16),
                pltpu.SemaphoreType.DMA((6,)),
            ],
        ),
        out_shape=[jax.ShapeDtypeStruct((ROWS, width), BF16) for width in widths],
        compiler_params=pltpu.CompilerParams(vmem_limit_bytes=58 * MIB),
        cost_estimate=pl.CostEstimate(flops=2**35, bytes_accessed=2**20, transcendentals=0),
        name="products",
    )(where, inverses, firsts, nexts, columns, *relay)


PIECES = (
    ((0, 0, 48, 0), (1, 0, 48, 48), (2, 0, 32, 96)),
    ((2, 32, 16, 0), (3, 0, 48, 16), (4, 0, 48, 64), (5, 0, 16, 112)),
    ((5, 16, 32, 0), (6, 0, 48, 32), (7, 0, 48, 80)),
)


def wanted_child(where_ref, target):
    found, child = jnp.int32(0), jnp.int32(0)
    for b in range(CHILD_BLOCKS):
        hit = (where_ref[2 + b] == target).astype(jnp.int32)
        found, child = found + hit, child + hit * b
    return found > 0, child


def carried_group(r):
    return jnp.where((r == 0) | (r == 3), 3, 2)


def join_kernel(where_ref, child_ref, half_ref, sems):
    r, z = where_ref[0], where_ref[1]
    found, child = wanted_child(where_ref, carried_group(r) * 8 + z)

    def copies(j):
        return [
            pltpu.make_async_copy(
                child_ref.at[z_from, pl.ds(part * CHILD_ROWS + start, rows), :],
                half_ref.at[pl.ds(place, rows), pl.ds(part * THIRD, THIRD)],
                sems.at[i, part],
            )
            for i, (z_from, start, rows, place) in enumerate(PIECES[j])
            for part in range(3)
        ]

    half_ref[...] = jnp.zeros_like(half_ref)
    for j in range(3):
        @pl.when(found & (child % 3 == j))
        def _():
            for copy in copies(j):
                copy.start()
            for copy in copies(j):
                copy.wait()


def join(where, children):
    return pl.pallas_call(
        join_kernel,
        grid_spec=pltpu.PrefetchScalarGridSpec(
            num_scalar_prefetch=1,
            grid=(1,),
            in_specs=[pl.BlockSpec(memory_space=pl.ANY)],
            out_specs=pl.BlockSpec((ROWS, HALF), lambda i, w: (0, 0)),
            scratch_shapes=[pltpu.SemaphoreType.DMA((4, 3))],
        ),
        out_shape=jax.ShapeDtypeStruct((ROWS, HALF), BF16),
        compiler_params=pltpu.CompilerParams(vmem_limit_bytes=8 * MIB),
        name="join",
    )(where, children)


def final_kernel(
    where_ref, front_ref, zero_ref, one_ref, two_ref, three_ref, across_groups_ref, left_ref, right_ref, schur_ref,
    held_ref, product_ref, block_ref, read_sems, child_sems, write_sems,
):
    r, z = where_ref[0], where_ref[1]
    found, _ = wanted_child(where_ref, r * 8 + z)
    halves = [
        pltpu.make_async_copy(ref, block_ref.at[:, pl.ds(half * HALF, HALF)], child_sems.at[half])
        for half, ref in enumerate((left_ref, right_ref))
    ]

    def read_front(g):
        place = pl.ds((g + 1) * GROUP, GROUP)
        return pltpu.make_async_copy(front_ref.at[0, :, place], held_ref.at[g], read_sems.at[0, g])

    def read_product(g, k):
        if k == 0:
            return [pltpu.make_async_copy(zero_ref, product_ref.at[g], read_sems.at[1, g])]
        sent = product_ref.at[g, :, pl.ds(0, SENT)]
        kept = product_ref.at[g, :, pl.ds(SENT, ROWS)]
        place = pl.ds((4 - k) * ROWS, ROWS)
        return [
            pltpu.make_async_copy((one_ref, two_ref, three_ref)[k - 1], sent, read_sems.at[1, g]),
            pltpu.make_async_copy(across_groups_ref.at[:, place], kept, read_sems.at[1, g]),
        ]

    def write(g):
        place = pl.ds(g * GROUP, GROUP)
        return pltpu.make_async_copy(held_ref.at[g], schur_ref.at[0, :, place], write_sems.at[g])

    for g in range(3):
        read_front(g).start()
        for k in range(4):
            @pl.when((r - g + 3) % 4 == k)
            def _():
                for copy in read_product(g, k):
                    copy.start()
    for copy in halves:
        copy.start()

    for g in range(3):
        read_front(g).wait()
        read_product(g, 0)[0].wait()
        for i in range(8):
            place = pl.ds(pl.multiple_of((z + 1 + i) % 8 * ROWS, ROWS), ROWS)
            held_ref[g, :, place] -= product_ref[g, :, i * ROWS : (i + 1) * ROWS].astype(F32)
        if g == 1:
            for copy in halves:
                copy.wait()
        if g >= 1:
            for b in range(CHILD_BLOCKS):
                parent = where_ref[2 + b]
                @pl.when(found & (parent // 8 == g + 1))
                def _():
                    place = pl.ds(pl.multiple_of((parent % 8) * ROWS, ROWS), ROWS)
                    held_ref[g, :, place] += block_ref[:, b * ROWS : (b + 1) * ROWS].astype(F32)
        write(g).start()
    for g in range(3):
        write(g).wait()


def final(where, assembled, pieces, halves):
    return pl.pallas_call(
        final_kernel,
        grid_spec=pltpu.PrefetchScalarGridSpec(
            num_scalar_prefetch=1,
            grid=(1,),
            in_specs=[pl.BlockSpec(memory_space=pl.ANY)] * 8,
            out_specs=pl.BlockSpec(memory_space=pl.ANY),
            scratch_shapes=[
                pltpu.VMEM((3, ROWS, GROUP), F32),
                pltpu.VMEM((3, ROWS, GROUP), BF16),
                pltpu.VMEM((ROWS, CHILD), BF16),
                pltpu.SemaphoreType.DMA((2, 3)),
                pltpu.SemaphoreType.DMA((2,)),
                pltpu.SemaphoreType.DMA((3,)),
            ],
        ),
        out_shape=jax.ShapeDtypeStruct((1, ROWS, 3 * GROUP), F32),
        compiler_params=pltpu.CompilerParams(vmem_limit_bytes=8 * MIB),
        name="final",
    )(where, assembled, *pieces, *halves)


def wanted_kernel(where_ref, parts_ref, out_ref, sems):
    group = carried_group(where_ref[0])
    copies = []
    for z in range(8):
        _, child = wanted_child(where_ref, group * 8 + z)
        source = parts_ref.at[jnp.minimum(child // 3, 3), pl.ds(2 * ROWS, 3 * CHILD_ROWS), :]
        copies.append(pltpu.make_async_copy(source, out_ref.at[z], sems.at[z]))
        copies[z].start()
    for copy in copies:
        copy.wait()


def wanted(where, parts):
    return pl.pallas_call(
        wanted_kernel,
        grid_spec=pltpu.PrefetchScalarGridSpec(
            num_scalar_prefetch=1,
            grid=(1,),
            in_specs=[pl.BlockSpec((4, PART_ROWS, THIRD), lambda i, w: (0, 0, 0))],
            out_specs=pl.BlockSpec(memory_space=pl.ANY),
            scratch_shapes=[pltpu.SemaphoreType.DMA((8,))],
        ),
        out_shape=jax.ShapeDtypeStruct((8, 3 * CHILD_ROWS, THIRD), BF16),
        compiler_params=pltpu.CompilerParams(vmem_limit_bytes=8 * MIB),
        name="wanted",
    )(where, parts)


def on_device(assembled, update, blocks, inverses):
    r, z = lax.axis_index("row"), lax.axis_index("col")
    where = jnp.concatenate([jnp.stack([r, z]).astype(jnp.int32), blocks[0]])

    both, first = first_panel(assembled, inverses)
    columns = lax.all_gather(both, "col", axis=0)
    first, update = lax.optimization_barrier((first, update))
    child = lax.ppermute(update[0], "front", [(i, i ^ 1) for i in range(16)])
    firsts = lax.all_gather(first, "row", axis=0)

    top = firsts[0]
    child, top = lax.optimization_barrier((child, top))
    parts = lax.all_to_all(pack(both, child), "row", 0, 0)
    passed = lax.ppermute(top, "col", [(4, 1), (5, 0), (6, 3), (7, 2)])
    mine = first_relay(where, passed, firsts)
    beside = lax.ppermute(mine, "col", [(i, i ^ 1) for i in range(8)])
    across = lax.ppermute(
        jnp.concatenate([mine, beside]),
        "col",
        [(i, (i + 1) % 8 if i % 2 else (i + 7) % 8) for i in range(8)],
    )
    relay = mine, beside, across
    pieces = wanted(where, parts)
    beside, pieces = lax.optimization_barrier((beside, pieces))
    children = lax.all_to_all(pieces, "col", 0, 0)

    zero, one, two, three, across_groups = products(where, inverses, firsts, parts, columns, relay)
    factor = own_factor(where, assembled, inverses, first, relay)
    two = lax.ppermute(two, "row", [(i, (i + 2) % 4) for i in range(1, 4)])
    one = lax.ppermute(one, "row", [(i, (i + 1) % 4) for i in range(1, 4)])
    three = lax.ppermute(three, "row", [(i, (i + 3) % 4) for i in range(1, 4)])
    pieces = zero, one, two, three, across_groups
    left = join(where, children)
    right = lax.ppermute(left, "row", [(1, 2), (0, 3)])
    return factor, final(where, assembled, pieces, (left, right))


def solution(mesh):
    return jax.shard_map(
        on_device,
        mesh=mesh,
        in_specs=(
            P("front", ("row", "col"), None),
            P("front", ("row", "col"), None),
            P("front", None),
            P("front", None, None, None),
        ),
        out_specs=(P("front", ("row", "col"), None), P("front", ("row", "col"), None)),
        check_vma=False,
    )
```

```python
import jax
import jax.numpy as jnp
from jax import lax
from jax.experimental import pallas as pl
from jax.experimental.pallas import tpu as pltpu
from jax.sharding import PartitionSpec as P

WIDTH = 512
ROWS = 128
GROUP = 1024
SENT = GROUP - ROWS
CHILD = 1536
CHILD_BLOCKS = 12
CHILD_ROWS = 48
HALF = CHILD // 2
THIRD = 256
PART_ROWS = 2 * ROWS + 3 * CHILD_ROWS
MIB = 1024 * 1024
VMEM_LIMIT = 60 * MIB

F32 = jnp.float32
BF16 = jnp.bfloat16


def dot(a, b):
    return jnp.dot(a, b, preferred_element_type=F32)


def dot_t(a, b):
    return lax.dot_general(a, b, (((1,), (1,)), ((), ())), preferred_element_type=F32)


def dot_split(a, b, terms):
    total = None
    for _ in range(terms):
        part = a.astype(BF16)
        a = a - part.astype(F32)
        product = dot(part, b)
        total = product if total is None else total + product
    return total


def upper(product, a, b):
    half = WIDTH // 2
    left = product(a[..., :half], b[:half, :half])
    return jnp.concatenate([left, product(a, b[:, half:])], axis=1)


def first_kernel(front_ref, inverse_ref, both_ref, first_ref):
    split = lambda a, b: dot_split(a, b, 3)
    first = upper(split, front_ref[0, :, :WIDTH], inverse_ref[0, 0]).astype(BF16)
    both_ref[:, :WIDTH] = first
    both_ref[:, WIDTH:] = front_ref[0, :, WIDTH:].astype(BF16)
    first_ref[...] = first


def first_panel(assembled, inverses):
    return pl.pallas_call(
        first_kernel,
        grid=(1,),
        in_specs=[
            pl.BlockSpec((1, ROWS, 2 * WIDTH), lambda i: (0, 0, 0)),
            pl.BlockSpec((1, 1, WIDTH, WIDTH), lambda i: (0, 0, 0, 0)),
        ],
        out_specs=[
            pl.BlockSpec((ROWS, 2 * WIDTH), lambda i: (0, 0)),
            pl.BlockSpec((ROWS, WIDTH), lambda i: (0, 0)),
        ],
        out_shape=[
            jax.ShapeDtypeStruct((ROWS, 2 * WIDTH), BF16),
            jax.ShapeDtypeStruct((ROWS, WIDTH), BF16),
        ],
        compiler_params=pltpu.CompilerParams(vmem_limit_bytes=VMEM_LIMIT),
        name="first_panel",
    )(assembled, inverses)


def pack_kernel(both_ref, child_ref, parts_ref):
    for k in range(4):
        for half in range(2):
            place = slice(half * ROWS, (half + 1) * ROWS)
            parts_ref[k, place] = both_ref[:, half * THIRD : (half + 1) * THIRD]
        first = 0 if k >= 2 else HALF
        for part in range(3):
            start = 2 * ROWS + part * CHILD_ROWS
            column = first + part * THIRD
            parts_ref[k, start : start + CHILD_ROWS] = child_ref[:, column : column + THIRD]


def pack(both, child):
    return pl.pallas_call(
        pack_kernel,
        grid=(1,),
        in_specs=[
            pl.BlockSpec((ROWS, WIDTH), lambda i: (0, 1)),
            pl.BlockSpec((CHILD_ROWS, CHILD), lambda i: (0, 0)),
        ],
        out_specs=pl.BlockSpec((4, PART_ROWS, THIRD), lambda i: (0, 0, 0)),
        out_shape=jax.ShapeDtypeStruct((4, PART_ROWS, THIRD), BF16),
        compiler_params=pltpu.CompilerParams(vmem_limit_bytes=8 * MIB),
        name="pack",
    )(both, child)


def piece_of(z):
    return jnp.where(z < 4, z ^ 1, z - 4)


def mine_kernel(where_ref, passed_ref, top_ref, mine_ref):
    mine_ref[...] = jnp.where(where_ref[1] < 4, passed_ref[...], top_ref[0])


def first_relay(where, passed, firsts):
    return pl.pallas_call(
        mine_kernel,
        grid_spec=pltpu.PrefetchScalarGridSpec(
            num_scalar_prefetch=1,
            grid=(1,),
            in_specs=[
                pl.BlockSpec((ROWS, WIDTH), lambda i, w: (0, 0)),
                pl.BlockSpec((1, ROWS, WIDTH), lambda i, w: (0, 0, 0)),
            ],
            out_specs=pl.BlockSpec((ROWS, WIDTH), lambda i, w: (0, 0)),
        ),
        out_shape=jax.ShapeDtypeStruct((ROWS, WIDTH), BF16),
        compiler_params=pltpu.CompilerParams(vmem_limit_bytes=8 * MIB),
        cost_estimate=pl.CostEstimate(flops=11_800_000_000, bytes_accessed=2**20, transcendentals=0),
        name="first_relay",
    )(where, passed, firsts)


def put_second(z, second_ref, mine_ref, beside_ref, across_ref):
    here, there = piece_of(z), piece_of((z + 2 * (z % 2) + 7) % 8)
    pieces = (
        (here, mine_ref[...]),
        (here ^ 1, beside_ref[...]),
        (there, across_ref[:ROWS]),
        (there ^ 1, across_ref[ROWS:]),
    )
    for piece, value in pieces:
        second_ref[pl.ds(pl.multiple_of(piece * ROWS, ROWS), ROWS), :] = value


def factor_kernel(
    where_ref, front_ref, inverse_ref, first_ref, mine_ref, beside_ref, across_ref, factor_ref, second_ref
):
    r, z = where_ref[0], where_ref[1]
    put_second(z, second_ref, mine_ref, beside_ref, across_ref)
    own = front_ref[0] - dot_t(first_ref[...], second_ref[...])
    own = dot_split(own, inverse_ref[0, 0], 3)
    own = jnp.where((r == 0) & (z < 4), jnp.zeros_like(own), own)
    factor_ref[0, :, :WIDTH] = first_ref[...]
    factor_ref[0, :, WIDTH:] = own.astype(BF16)


def own_factor(where, assembled, inverses, first, relay):
    whole = lambda *shape: pl.BlockSpec(shape, lambda i, w: (0,) * len(shape))
    return pl.pallas_call(
        factor_kernel,
        grid_spec=pltpu.PrefetchScalarGridSpec(
            num_scalar_prefetch=1,
            grid=(1,),
            in_specs=[
                pl.BlockSpec((1, ROWS, WIDTH), lambda i, w: (0, 0, 1)),
                pl.BlockSpec((1, 1, WIDTH, WIDTH), lambda i, w: (0, 1, 0, 0)),
                whole(ROWS, WIDTH),
                whole(ROWS, WIDTH),
                whole(ROWS, WIDTH),
                whole(2 * ROWS, WIDTH),
            ],
            out_specs=whole(1, ROWS, 2 * WIDTH),
            scratch_shapes=[pltpu.VMEM((WIDTH, WIDTH), BF16)],
        ),
        out_shape=jax.ShapeDtypeStruct((1, ROWS, 2 * WIDTH), BF16),
        compiler_params=pltpu.CompilerParams(vmem_limit_bytes=8 * MIB),
        cost_estimate=pl.CostEstimate(flops=2**28, bytes_accessed=2**21, transcendentals=0),
        name="own_factor",
    )(where, assembled, inverses, first, *relay)


def product_kernel(
    where_ref, inverse_ref, firsts_ref, nexts_ref, column_ref, mine_ref, beside_ref, across_ref,
    zero_ref, one_ref, two_ref, three_ref, across_groups_ref,
    held_inverse_ref, second_ref, weight_ref, rows_ref, next_ref, columns_ref, following_ref, sems,
):
    r, z = where_ref[0], where_ref[1]

    def rows_at(place):
        return pl.ds(pl.multiple_of(place * ROWS, ROWS), ROWS)

    def await_all(ref, sem):
        pltpu.make_async_copy(ref, ref, sem).wait()

    here, there = piece_of(z), piece_of((z + 2 * (z % 2) + 7) % 8)
    pieces = (
        (here, mine_ref),
        (here ^ 1, beside_ref),
        (there, across_ref.at[:ROWS]),
        (there ^ 1, across_ref.at[ROWS:]),
    )
    for place, ref in pieces:
        pltpu.make_async_copy(ref, second_ref.at[rows_at(place)], sems.at[0]).start()
    pltpu.make_async_copy(inverse_ref.at[0, 1], held_inverse_ref, sems.at[1]).start()
    for k in range(4):
        place = rows_at((k - r + 4) % 4)
        part = rows_ref.at[place, pl.ds(0, WIDTH)]
        pltpu.make_async_copy(firsts_ref.at[k], part, sems.at[2]).start()
        for half in range(2):
            source = nexts_ref.at[k, pl.ds(half * ROWS, ROWS), :]
            part = next_ref.at[place, pl.ds(half * THIRD, THIRD)]
            pltpu.make_async_copy(source, part, sems.at[3]).start()
    for j in range(8):
        place = rows_at((j - z + 7) % 8)
        part = column_ref.at[j, :, pl.ds(0, WIDTH)]
        pltpu.make_async_copy(part, columns_ref.at[place, pl.ds(0, WIDTH)], sems.at[4]).start()
        part = column_ref.at[j, :, pl.ds(WIDTH, WIDTH)]
        pltpu.make_async_copy(part, following_ref.at[place], sems.at[5]).start()

    await_all(second_ref, sems.at[0])
    await_all(held_inverse_ref, sems.at[1])
    inverse = held_inverse_ref[...]
    turned = lax.dot_general(
        second_ref[...], inverse, (((0,), (0,)), ((), ())), preferred_element_type=F32
    )
    high = turned.astype(BF16)
    weight_ref[0] = high
    weight_ref[1] = (turned - high.astype(F32)).astype(BF16)

    def panel_of(first, following):
        lost = dot(first, weight_ref[0]) + dot(first, weight_ref[1])
        return upper(dot, following, inverse) - lost

    await_all(rows_ref.at[:, pl.ds(0, WIDTH)], sems.at[2])
    await_all(next_ref, sems.at[3])
    panel = panel_of(rows_ref[ROWS:, :WIDTH], next_ref[ROWS:, :])
    above = lax.broadcasted_iota(jnp.int32, (3 * ROWS, WIDTH), 0) // ROWS == jnp.where(z < 4, 3 - r, 4)
    rows_ref[ROWS:, WIDTH:] = jnp.where(above, jnp.zeros_like(panel), panel).astype(BF16)
    await_all(columns_ref.at[:, pl.ds(0, WIDTH)], sems.at[4])
    await_all(following_ref, sems.at[5])
    for half in range(2):
        place = pl.ds(half * 4 * ROWS, 4 * ROWS)
        panel = panel_of(columns_ref[place, :WIDTH], following_ref[place, :])
        if half == 1:
            last = lax.broadcasted_iota(jnp.int32, (4 * ROWS, WIDTH), 0) // ROWS
            above = last == jnp.where((r == 0) & (z < 4), 3, 4)
            panel = jnp.where(above, jnp.zeros_like(panel), panel)
        columns_ref[place, WIDTH:] = panel.astype(BF16)
    rows_ref[:ROWS, WIDTH:] = columns_ref[7 * ROWS :, WIDTH:]
    for part in range(4):
        place = pl.ds(part * 256, 256)
        exact = dot_t(rows_ref[...], columns_ref[place, :])
        total = exact.astype(BF16)
        zero_ref[:, place] = total[:ROWS]
        width = min(256, SENT - part * 256)
        for k, ref in enumerate((one_ref, two_ref, three_ref), 1):
            ref[:, part * 256 : part * 256 + width] = total[k * ROWS : (k + 1) * ROWS, :width]
    for k in range(4):
        place = slice(k * ROWS, (k + 1) * ROWS)
        across_groups_ref[:, place] = exact[place, ROWS:].T.astype(BF16)


def products(where, inverses, firsts, nexts, columns, relay):
    whole = lambda *shape: pl.BlockSpec(shape, lambda i, w: (0,) * len(shape))
    widths = GROUP, SENT, SENT, SENT, 4 * ROWS
    return pl.pallas_call(
        product_kernel,
        grid_spec=pltpu.PrefetchScalarGridSpec(
            num_scalar_prefetch=1,
            grid=(1,),
            in_specs=[pl.BlockSpec(memory_space=pl.ANY)] * 7,
            out_specs=[whole(ROWS, width) for width in widths],
            scratch_shapes=[
                pltpu.VMEM((WIDTH, WIDTH), BF16),
                pltpu.VMEM((WIDTH, WIDTH), BF16),
                pltpu.VMEM((2, WIDTH, WIDTH), BF16),
                pltpu.VMEM((4 * ROWS, 2 * WIDTH), BF16),
                pltpu.VMEM((4 * ROWS, WIDTH), BF16),
                pltpu.VMEM((8 * ROWS, 2 * WIDTH), BF16),
                pltpu.VMEM((8 * ROWS, WIDTH), BF16),
                pltpu.SemaphoreType.DMA((6,)),
            ],
        ),
        out_shape=[jax.ShapeDtypeStruct((ROWS, width), BF16) for width in widths],
        compiler_params=pltpu.CompilerParams(vmem_limit_bytes=58 * MIB),
        cost_estimate=pl.CostEstimate(flops=2**35, bytes_accessed=2**20, transcendentals=0),
        name="products",
    )(where, inverses, firsts, nexts, columns, *relay)


PIECES = (
    ((0, 0, 48, 0), (1, 0, 48, 48), (2, 0, 32, 96)),
    ((2, 32, 16, 0), (3, 0, 48, 16), (4, 0, 48, 64), (5, 0, 16, 112)),
    ((5, 16, 32, 0), (6, 0, 48, 32), (7, 0, 48, 80)),
)


def wanted_child(where_ref, target):
    found, child = jnp.int32(0), jnp.int32(0)
    for b in range(CHILD_BLOCKS):
        hit = (where_ref[2 + b] == target).astype(jnp.int32)
        found, child = found + hit, child + hit * b
    return found > 0, child


def carried_group(r):
    return jnp.where((r == 0) | (r == 3), 3, 2)


def join_kernel(where_ref, child_ref, half_ref, sems):
    r, z = where_ref[0], where_ref[1]
    found, child = wanted_child(where_ref, carried_group(r) * 8 + z)

    def copies(j):
        return [
            pltpu.make_async_copy(
                child_ref.at[z_from, pl.ds(part * CHILD_ROWS + start, rows), :],
                half_ref.at[pl.ds(place, rows), pl.ds(part * THIRD, THIRD)],
                sems.at[i, part],
            )
            for i, (z_from, start, rows, place) in enumerate(PIECES[j])
            for part in range(3)
        ]

    half_ref[...] = jnp.zeros_like(half_ref)
    for j in range(3):
        @pl.when(found & (child % 3 == j))
        def _():
            for copy in copies(j):
                copy.start()
            for copy in copies(j):
                copy.wait()


def join(where, children):
    return pl.pallas_call(
        join_kernel,
        grid_spec=pltpu.PrefetchScalarGridSpec(
            num_scalar_prefetch=1,
            grid=(1,),
            in_specs=[pl.BlockSpec(memory_space=pl.ANY)],
            out_specs=pl.BlockSpec((ROWS, HALF), lambda i, w: (0, 0)),
            scratch_shapes=[pltpu.SemaphoreType.DMA((4, 3))],
        ),
        out_shape=jax.ShapeDtypeStruct((ROWS, HALF), BF16),
        compiler_params=pltpu.CompilerParams(vmem_limit_bytes=8 * MIB),
        name="join",
    )(where, children)


def final_kernel(
    where_ref, front_ref, zero_ref, one_ref, two_ref, three_ref, across_groups_ref, left_ref, right_ref, schur_ref,
    held_ref, product_ref, block_ref, read_sems, child_sems, write_sems,
):
    r, z = where_ref[0], where_ref[1]
    found, _ = wanted_child(where_ref, r * 8 + z)
    halves = [
        pltpu.make_async_copy(ref, block_ref.at[:, pl.ds(half * HALF, HALF)], child_sems.at[half])
        for half, ref in enumerate((left_ref, right_ref))
    ]

    def read_front(g):
        place = pl.ds((g + 1) * GROUP, GROUP)
        return pltpu.make_async_copy(front_ref.at[0, :, place], held_ref.at[g], read_sems.at[0, g])

    def read_product(g, k):
        if k == 0:
            return [pltpu.make_async_copy(zero_ref, product_ref.at[g], read_sems.at[1, g])]
        sent = product_ref.at[g, :, pl.ds(0, SENT)]
        kept = product_ref.at[g, :, pl.ds(SENT, ROWS)]
        place = pl.ds((4 - k) * ROWS, ROWS)
        return [
            pltpu.make_async_copy((one_ref, two_ref, three_ref)[k - 1], sent, read_sems.at[1, g]),
            pltpu.make_async_copy(across_groups_ref.at[:, place], kept, read_sems.at[1, g]),
        ]

    def write(g):
        place = pl.ds(g * GROUP, GROUP)
        return pltpu.make_async_copy(held_ref.at[g], schur_ref.at[0, :, place], write_sems.at[g])

    for g in range(3):
        read_front(g).start()
        for k in range(4):
            @pl.when((r - g + 3) % 4 == k)
            def _():
                for copy in read_product(g, k):
                    copy.start()
    for copy in halves:
        copy.start()

    for g in range(3):
        read_front(g).wait()
        read_product(g, 0)[0].wait()
        for i in range(8):
            place = pl.ds(pl.multiple_of((z + 1 + i) % 8 * ROWS, ROWS), ROWS)
            held_ref[g, :, place] -= product_ref[g, :, i * ROWS : (i + 1) * ROWS].astype(F32)
        if g == 1:
            for copy in halves:
                copy.wait()
        if g >= 1:
            for b in range(CHILD_BLOCKS):
                parent = where_ref[2 + b]
                @pl.when(found & (parent // 8 == g + 1))
                def _():
                    place = pl.ds(pl.multiple_of((parent % 8) * ROWS, ROWS), ROWS)
                    held_ref[g, :, place] += block_ref[:, b * ROWS : (b + 1) * ROWS].astype(F32)
        write(g).start()
    for g in range(3):
        write(g).wait()


def final(where, assembled, pieces, halves):
    return pl.pallas_call(
        final_kernel,
        grid_spec=pltpu.PrefetchScalarGridSpec(
            num_scalar_prefetch=1,
            grid=(1,),
            in_specs=[pl.BlockSpec(memory_space=pl.ANY)] * 8,
            out_specs=pl.BlockSpec(memory_space=pl.ANY),
            scratch_shapes=[
                pltpu.VMEM((3, ROWS, GROUP), F32),
                pltpu.VMEM((3, ROWS, GROUP), BF16),
                pltpu.VMEM((ROWS, CHILD), BF16),
                pltpu.SemaphoreType.DMA((2, 3)),
                pltpu.SemaphoreType.DMA((2,)),
                pltpu.SemaphoreType.DMA((3,)),
            ],
        ),
        out_shape=jax.ShapeDtypeStruct((1, ROWS, 3 * GROUP), F32),
        compiler_params=pltpu.CompilerParams(vmem_limit_bytes=8 * MIB),
        name="final",
    )(where, assembled, *pieces, *halves)


def wanted_kernel(where_ref, parts_ref, out_ref, sems):
    group = carried_group(where_ref[0])
    copies = []
    for z in range(8):
        _, child = wanted_child(where_ref, group * 8 + z)
        source = parts_ref.at[jnp.minimum(child // 3, 3), pl.ds(2 * ROWS, 3 * CHILD_ROWS), :]
        copies.append(pltpu.make_async_copy(source, out_ref.at[z], sems.at[z]))
        copies[z].start()
    for copy in copies:
        copy.wait()


def wanted(where, parts):
    return pl.pallas_call(
        wanted_kernel,
        grid_spec=pltpu.PrefetchScalarGridSpec(
            num_scalar_prefetch=1,
            grid=(1,),
            in_specs=[pl.BlockSpec((4, PART_ROWS, THIRD), lambda i, w: (0, 0, 0))],
            out_specs=pl.BlockSpec(memory_space=pl.ANY),
            scratch_shapes=[pltpu.SemaphoreType.DMA((8,))],
        ),
        out_shape=jax.ShapeDtypeStruct((8, 3 * CHILD_ROWS, THIRD), BF16),
        compiler_params=pltpu.CompilerParams(vmem_limit_bytes=8 * MIB),
        name="wanted",
    )(where, parts)


def on_device(assembled, update, blocks, inverses):
    r, z = lax.axis_index("row"), lax.axis_index("col")
    where = jnp.concatenate([jnp.stack([r, z]).astype(jnp.int32), blocks[0]])

    both, first = first_panel(assembled, inverses)
    columns = lax.all_gather(both, "col", axis=0)
    first, update = lax.optimization_barrier((first, update))
    child = lax.ppermute(update[0], "front", [(i, i ^ 1) for i in range(16)])
    firsts = lax.all_gather(first, "row", axis=0)

    top = firsts[0]
    child, top = lax.optimization_barrier((child, top))
    parts = lax.all_to_all(pack(both, child), "row", 0, 0)
    passed = lax.ppermute(top, "col", [(4, 1), (5, 0), (6, 3), (7, 2)])
    mine = first_relay(where, passed, firsts)
    beside = lax.ppermute(mine, "col", [(i, i ^ 1) for i in range(8)])
    across = lax.ppermute(
        jnp.concatenate([mine, beside]),
        "col",
        [(i, (i + 1) % 8 if i % 2 else (i + 7) % 8) for i in range(8)],
    )
    relay = mine, beside, across
    pieces = wanted(where, parts)
    beside, pieces = lax.optimization_barrier((beside, pieces))
    children = lax.all_to_all(pieces, "col", 0, 0)

    zero, one, two, three, across_groups = products(where, inverses, firsts, parts, columns, relay)
    factor = own_factor(where, assembled, inverses, first, relay)
    two = lax.ppermute(two, "row", [(i, (i + 2) % 4) for i in range(1, 4)])
    one = lax.ppermute(one, "row", [(i, (i + 1) % 4) for i in range(1, 4)])
    three = lax.ppermute(three, "row", [(i, (i + 3) % 4) for i in range(1, 4)])
    pieces = zero, one, two, three, across_groups
    left = join(where, children)
    right = lax.ppermute(left, "row", [(1, 2), (0, 3)])
    return factor, final(where, assembled, pieces, (left, right))


def solution(mesh):
    return jax.shard_map(
        on_device,
        mesh=mesh,
        in_specs=(
            P("front", ("row", "col"), None),
            P("front", ("row", "col"), None),
            P("front", None),
            P("front", None, None, None),
        ),
        out_specs=(P("front", ("row", "col"), None), P("front", ("row", "col"), None)),
        check_vma=False,
    )
```

```python
import jax
import jax.numpy as jnp
from jax import lax
from jax.experimental import pallas as pl
from jax.experimental.pallas import tpu as pltpu
from jax.sharding import PartitionSpec as P

WIDTH = 512
ROWS = 128
GROUP = 1024
SENT = GROUP - ROWS
CHILD = 1536
CHILD_BLOCKS = 12
CHILD_ROWS = 48
KEPT = 1024
LENT = CHILD - KEPT
THIRD = 256
PART_ROWS = 2 * ROWS + 4 * CHILD_ROWS
MIB = 1024 * 1024
VMEM_LIMIT = 60 * MIB

F32 = jnp.float32
BF16 = jnp.bfloat16


def dot(a, b):
    return jnp.dot(a, b, preferred_element_type=F32)


def dot_t(a, b):
    return lax.dot_general(a, b, (((1,), (1,)), ((), ())), preferred_element_type=F32)


def dot_split(a, b, terms):
    total = None
    for _ in range(terms):
        part = a.astype(BF16)
        a = a - part.astype(F32)
        product = dot(part, b)
        total = product if total is None else total + product
    return total


def first_kernel(front_ref, inverse_ref, both_ref, first_ref):
    first = dot_split(front_ref[0, :, :WIDTH], inverse_ref[0, 0], 3).astype(BF16)
    both_ref[:, :WIDTH] = first
    both_ref[:, WIDTH:] = front_ref[0, :, WIDTH:].astype(BF16)
    first_ref[...] = first


def first_panel(assembled, inverses):
    return pl.pallas_call(
        first_kernel,
        grid=(1,),
        in_specs=[
            pl.BlockSpec((1, ROWS, 2 * WIDTH), lambda i: (0, 0, 0)),
            pl.BlockSpec((1, 1, WIDTH, WIDTH), lambda i: (0, 0, 0, 0)),
        ],
        out_specs=[
            pl.BlockSpec((ROWS, 2 * WIDTH), lambda i: (0, 0)),
            pl.BlockSpec((ROWS, WIDTH), lambda i: (0, 0)),
        ],
        out_shape=[
            jax.ShapeDtypeStruct((ROWS, 2 * WIDTH), BF16),
            jax.ShapeDtypeStruct((ROWS, WIDTH), BF16),
        ],
        compiler_params=pltpu.CompilerParams(vmem_limit_bytes=VMEM_LIMIT),
        name="first_panel",
    )(assembled, inverses)


def pack_kernel(both_ref, child_ref, parts_ref):
    for k in range(4):
        for half in range(2):
            place = slice(half * ROWS, (half + 1) * ROWS)
            parts_ref[k, place] = both_ref[:, half * THIRD : (half + 1) * THIRD]
        for part in range(4):
            start = 2 * ROWS + part * CHILD_ROWS
            column = part * THIRD if k >= 2 else KEPT + part % 2 * THIRD
            parts_ref[k, start : start + CHILD_ROWS] = child_ref[:, column : column + THIRD]


def pack(both, child):
    return pl.pallas_call(
        pack_kernel,
        grid=(1,),
        in_specs=[
            pl.BlockSpec((ROWS, WIDTH), lambda i: (0, 1)),
            pl.BlockSpec((CHILD_ROWS, CHILD), lambda i: (0, 0)),
        ],
        out_specs=pl.BlockSpec((4, PART_ROWS, THIRD), lambda i: (0, 0, 0)),
        out_shape=jax.ShapeDtypeStruct((4, PART_ROWS, THIRD), BF16),
        compiler_params=pltpu.CompilerParams(vmem_limit_bytes=8 * MIB),
        name="pack",
    )(both, child)


def piece_of(z):
    return jnp.where(z < 4, z ^ 1, z - 4)


def mine_kernel(where_ref, passed_ref, top_ref, mine_ref):
    mine_ref[...] = jnp.where(where_ref[1] < 4, passed_ref[...], top_ref[0])


def first_relay(where, passed, firsts):
    return pl.pallas_call(
        mine_kernel,
        grid_spec=pltpu.PrefetchScalarGridSpec(
            num_scalar_prefetch=1,
            grid=(1,),
            in_specs=[
                pl.BlockSpec((ROWS, WIDTH), lambda i, w: (0, 0)),
                pl.BlockSpec((1, ROWS, WIDTH), lambda i, w: (0, 0, 0)),
            ],
            out_specs=pl.BlockSpec((ROWS, WIDTH), lambda i, w: (0, 0)),
        ),
        out_shape=jax.ShapeDtypeStruct((ROWS, WIDTH), BF16),
        compiler_params=pltpu.CompilerParams(vmem_limit_bytes=8 * MIB),
        cost_estimate=pl.CostEstimate(flops=11_800_000_000, bytes_accessed=2**20, transcendentals=0),
        name="first_relay",
    )(where, passed, firsts)


def put_second(z, second_ref, mine_ref, beside_ref, across_ref):
    here, there = piece_of(z), piece_of((z + 2 * (z % 2) + 7) % 8)
    pieces = (
        (here, mine_ref[...]),
        (here ^ 1, beside_ref[...]),
        (there, across_ref[:ROWS]),
        (there ^ 1, across_ref[ROWS:]),
    )
    for piece, value in pieces:
        second_ref[pl.ds(pl.multiple_of(piece * ROWS, ROWS), ROWS), :] = value


def factor_kernel(
    where_ref, front_ref, inverse_ref, first_ref, mine_ref, beside_ref, across_ref, factor_ref, second_ref
):
    r, z = where_ref[0], where_ref[1]
    put_second(z, second_ref, mine_ref, beside_ref, across_ref)
    own = front_ref[0] - dot_t(first_ref[...], second_ref[...])
    own = dot_split(own, inverse_ref[0, 0], 3)
    own = jnp.where((r == 0) & (z < 4), jnp.zeros_like(own), own)
    factor_ref[0, :, :WIDTH] = first_ref[...]
    factor_ref[0, :, WIDTH:] = own.astype(BF16)


def own_factor(where, assembled, inverses, first, relay):
    whole = lambda *shape: pl.BlockSpec(shape, lambda i, w: (0,) * len(shape))
    return pl.pallas_call(
        factor_kernel,
        grid_spec=pltpu.PrefetchScalarGridSpec(
            num_scalar_prefetch=1,
            grid=(1,),
            in_specs=[
                pl.BlockSpec((1, ROWS, WIDTH), lambda i, w: (0, 0, 1)),
                pl.BlockSpec((1, 1, WIDTH, WIDTH), lambda i, w: (0, 1, 0, 0)),
                whole(ROWS, WIDTH),
                whole(ROWS, WIDTH),
                whole(ROWS, WIDTH),
                whole(2 * ROWS, WIDTH),
            ],
            out_specs=whole(1, ROWS, 2 * WIDTH),
            scratch_shapes=[pltpu.VMEM((WIDTH, WIDTH), BF16)],
        ),
        out_shape=jax.ShapeDtypeStruct((1, ROWS, 2 * WIDTH), BF16),
        compiler_params=pltpu.CompilerParams(vmem_limit_bytes=8 * MIB),
        cost_estimate=pl.CostEstimate(flops=2**28, bytes_accessed=2**21, transcendentals=0),
        name="own_factor",
    )(where, assembled, inverses, first, *relay)


def product_kernel(
    where_ref, inverse_ref, firsts_ref, nexts_ref, column_ref, mine_ref, beside_ref, across_ref,
    zero_ref, one_ref, two_ref, three_ref, across_groups_ref,
    held_inverse_ref, second_ref, weight_ref, rows_ref, next_ref, columns_ref, following_ref, sems,
):
    r, z = where_ref[0], where_ref[1]

    def rows_at(place):
        return pl.ds(pl.multiple_of(place * ROWS, ROWS), ROWS)

    def await_all(ref, sem):
        pltpu.make_async_copy(ref, ref, sem).wait()

    here, there = piece_of(z), piece_of((z + 2 * (z % 2) + 7) % 8)
    pieces = (
        (here, mine_ref),
        (here ^ 1, beside_ref),
        (there, across_ref.at[:ROWS]),
        (there ^ 1, across_ref.at[ROWS:]),
    )
    for place, ref in pieces:
        pltpu.make_async_copy(ref, second_ref.at[rows_at(place)], sems.at[0]).start()
    pltpu.make_async_copy(inverse_ref.at[0, 1], held_inverse_ref, sems.at[1]).start()
    for k in range(4):
        place = rows_at((k - r + 4) % 4)
        part = rows_ref.at[place, pl.ds(0, WIDTH)]
        pltpu.make_async_copy(firsts_ref.at[k], part, sems.at[2]).start()
        for half in range(2):
            source = nexts_ref.at[k, pl.ds(half * ROWS, ROWS), :]
            part = next_ref.at[place, pl.ds(half * THIRD, THIRD)]
            pltpu.make_async_copy(source, part, sems.at[3]).start()
    for j in range(8):
        place = rows_at((j - z + 7) % 8)
        part = column_ref.at[j, :, pl.ds(0, WIDTH)]
        pltpu.make_async_copy(part, columns_ref.at[place, pl.ds(0, WIDTH)], sems.at[4]).start()
        part = column_ref.at[j, :, pl.ds(WIDTH, WIDTH)]
        pltpu.make_async_copy(part, following_ref.at[place], sems.at[5]).start()

    await_all(second_ref, sems.at[0])
    await_all(held_inverse_ref, sems.at[1])
    inverse = held_inverse_ref[...]
    turned = lax.dot_general(
        second_ref[...], inverse, (((0,), (0,)), ((), ())), preferred_element_type=F32
    )
    high = turned.astype(BF16)
    weight_ref[0] = high
    weight_ref[1] = (turned - high.astype(F32)).astype(BF16)

    def panel_of(first, following):
        lost = dot(first, weight_ref[0]) + dot(first, weight_ref[1])
        return dot(following, inverse) - lost

    await_all(rows_ref.at[:, pl.ds(0, WIDTH)], sems.at[2])
    await_all(next_ref, sems.at[3])
    panel = panel_of(rows_ref[:, :WIDTH], next_ref[...])
    top = jnp.where(z < 4, (4 - r) % 4, 4)
    above = lax.broadcasted_iota(jnp.int32, (4 * ROWS, WIDTH), 0) // ROWS == top
    rows_ref[:, WIDTH:] = jnp.where(above, jnp.zeros_like(panel), panel).astype(BF16)
    await_all(columns_ref.at[:, pl.ds(0, WIDTH)], sems.at[4])
    await_all(following_ref, sems.at[5])
    for half in range(2):
        place = pl.ds(half * 4 * ROWS, 4 * ROWS)
        panel = panel_of(columns_ref[place, :WIDTH], following_ref[place, :])
        columns_ref[place, WIDTH:] = panel.astype(BF16)
    for part in range(4):
        place = pl.ds(part * 256, 256)
        total = dot_t(rows_ref[...], columns_ref[place, :]).astype(BF16)
        zero_ref[:, place] = total[:ROWS]
        width = min(256, SENT - part * 256)
        for k, ref in enumerate((one_ref, two_ref, three_ref), 1):
            ref[:, part * 256 : part * 256 + width] = total[k * ROWS : (k + 1) * ROWS, :width]
    across_groups_ref[...] = dot_t(rows_ref[:ROWS, :], rows_ref[...]).astype(BF16)


def products(where, inverses, firsts, nexts, columns, relay):
    whole = lambda *shape: pl.BlockSpec(shape, lambda i, w: (0,) * len(shape))
    widths = GROUP, SENT, SENT, SENT, 4 * ROWS
    return pl.pallas_call(
        product_kernel,
        grid_spec=pltpu.PrefetchScalarGridSpec(
            num_scalar_prefetch=1,
            grid=(1,),
            in_specs=[pl.BlockSpec(memory_space=pl.ANY)] * 7,
            out_specs=[whole(ROWS, width) for width in widths],
            scratch_shapes=[
                pltpu.VMEM((WIDTH, WIDTH), BF16),
                pltpu.VMEM((WIDTH, WIDTH), BF16),
                pltpu.VMEM((2, WIDTH, WIDTH), BF16),
                pltpu.VMEM((4 * ROWS, 2 * WIDTH), BF16),
                pltpu.VMEM((4 * ROWS, WIDTH), BF16),
                pltpu.VMEM((8 * ROWS, 2 * WIDTH), BF16),
                pltpu.VMEM((8 * ROWS, WIDTH), BF16),
                pltpu.SemaphoreType.DMA((6,)),
            ],
        ),
        out_shape=[jax.ShapeDtypeStruct((ROWS, width), BF16) for width in widths],
        compiler_params=pltpu.CompilerParams(vmem_limit_bytes=58 * MIB),
        cost_estimate=pl.CostEstimate(flops=2**35, bytes_accessed=2**20, transcendentals=0),
        name="products",
    )(where, inverses, firsts, nexts, columns, *relay)


PIECES = (
    ((0, 0, 48, 0), (1, 0, 48, 48), (2, 0, 32, 96)),
    ((2, 32, 16, 0), (3, 0, 48, 16), (4, 0, 48, 64), (5, 0, 16, 112)),
    ((5, 16, 32, 0), (6, 0, 48, 32), (7, 0, 48, 80)),
)


def wanted_child(where_ref, target):
    found, child = jnp.int32(0), jnp.int32(0)
    for b in range(CHILD_BLOCKS):
        hit = (where_ref[2 + b] == target).astype(jnp.int32)
        found, child = found + hit, child + hit * b
    return found > 0, child


def carried_group(r):
    return jnp.where((r == 0) | (r == 3), 3, 2)


def join_kernel(where_ref, child_ref, half_ref, lent_ref, sems):
    r, z = where_ref[0], where_ref[1]
    found, child = wanted_child(where_ref, carried_group(r) * 8 + z)

    def copies(j):
        return [
            pltpu.make_async_copy(
                child_ref.at[z_from, pl.ds(part * CHILD_ROWS + start, rows), :],
                half_ref.at[pl.ds(place, rows), pl.ds(part * THIRD, THIRD)],
                sems.at[i, part],
            )
            for i, (z_from, start, rows, place) in enumerate(PIECES[j])
            for part in range(4)
        ]

    half_ref[...] = jnp.zeros_like(half_ref)
    for j in range(3):
        @pl.when(found & (child % 3 == j))
        def _():
            for copy in copies(j):
                copy.start()
            for copy in copies(j):
                copy.wait()
    lent_ref[...] = half_ref[:, :LENT]


def join(where, children):
    return pl.pallas_call(
        join_kernel,
        grid_spec=pltpu.PrefetchScalarGridSpec(
            num_scalar_prefetch=1,
            grid=(1,),
            in_specs=[pl.BlockSpec(memory_space=pl.ANY)],
            out_specs=[pl.BlockSpec((ROWS, width), lambda i, w: (0, 0)) for width in (KEPT, LENT)],
            scratch_shapes=[pltpu.SemaphoreType.DMA((4, 4))],
        ),
        out_shape=[jax.ShapeDtypeStruct((ROWS, width), BF16) for width in (KEPT, LENT)],
        compiler_params=pltpu.CompilerParams(vmem_limit_bytes=8 * MIB),
        name="join",
    )(where, children)


def final_kernel(
    where_ref, front_ref, zero_ref, one_ref, two_ref, three_ref, across_groups_ref, left_ref, right_ref, schur_ref,
    held_ref, product_ref, block_ref, read_sems, child_sems, write_sems,
):
    r, z = where_ref[0], where_ref[1]
    found, _ = wanted_child(where_ref, r * 8 + z)
    halves = [
        pltpu.make_async_copy(left_ref, block_ref.at[:, pl.ds(0, KEPT)], child_sems.at[0]),
        pltpu.make_async_copy(right_ref, block_ref.at[:, pl.ds(KEPT, LENT)], child_sems.at[1]),
    ]

    def read_front(g):
        place = pl.ds((g + 1) * GROUP, GROUP)
        return pltpu.make_async_copy(front_ref.at[0, :, place], held_ref.at[g], read_sems.at[0, g])

    def read_product(g, k):
        if k == 0:
            return [pltpu.make_async_copy(zero_ref, product_ref.at[g], read_sems.at[1, g])]
        sent = product_ref.at[g, :, pl.ds(0, SENT)]
        kept = product_ref.at[g, :, pl.ds(SENT, ROWS)]
        place = pl.ds((4 - k) * ROWS, ROWS)
        return [
            pltpu.make_async_copy((one_ref, two_ref, three_ref)[k - 1], sent, read_sems.at[1, g]),
            pltpu.make_async_copy(across_groups_ref.at[:, place], kept, read_sems.at[1, g]),
        ]

    def write(g):
        place = pl.ds(g * GROUP, GROUP)
        return pltpu.make_async_copy(held_ref.at[g], schur_ref.at[0, :, place], write_sems.at[g])

    for g in range(3):
        read_front(g).start()
        for k in range(4):
            @pl.when((r - g + 3) % 4 == k)
            def _():
                for copy in read_product(g, k):
                    copy.start()
    for copy in halves:
        copy.start()

    for g in range(3):
        read_front(g).wait()
        read_product(g, 0)[0].wait()
        for i in range(8):
            place = pl.ds(pl.multiple_of((z + 1 + i) % 8 * ROWS, ROWS), ROWS)
            held_ref[g, :, place] -= product_ref[g, :, i * ROWS : (i + 1) * ROWS].astype(F32)
        if g == 1:
            for copy in halves:
                copy.wait()
        if g >= 1:
            for b in range(CHILD_BLOCKS):
                parent = where_ref[2 + b]
                @pl.when(found & (parent // 8 == g + 1))
                def _():
                    place = pl.ds(pl.multiple_of((parent % 8) * ROWS, ROWS), ROWS)
                    held_ref[g, :, place] += block_ref[:, b * ROWS : (b + 1) * ROWS].astype(F32)
        write(g).start()
    for g in range(3):
        write(g).wait()


def final(where, assembled, pieces, halves):
    return pl.pallas_call(
        final_kernel,
        grid_spec=pltpu.PrefetchScalarGridSpec(
            num_scalar_prefetch=1,
            grid=(1,),
            in_specs=[pl.BlockSpec(memory_space=pl.ANY)] * 8,
            out_specs=pl.BlockSpec(memory_space=pl.ANY),
            scratch_shapes=[
                pltpu.VMEM((3, ROWS, GROUP), F32),
                pltpu.VMEM((3, ROWS, GROUP), BF16),
                pltpu.VMEM((ROWS, CHILD), BF16),
                pltpu.SemaphoreType.DMA((2, 3)),
                pltpu.SemaphoreType.DMA((2,)),
                pltpu.SemaphoreType.DMA((3,)),
            ],
        ),
        out_shape=jax.ShapeDtypeStruct((1, ROWS, 3 * GROUP), F32),
        compiler_params=pltpu.CompilerParams(vmem_limit_bytes=8 * MIB),
        name="final",
    )(where, assembled, *pieces, *halves)


def wanted_kernel(where_ref, parts_ref, out_ref, sems):
    group = carried_group(where_ref[0])
    copies = []
    for z in range(8):
        _, child = wanted_child(where_ref, group * 8 + z)
        source = parts_ref.at[jnp.minimum(child // 3, 3), pl.ds(2 * ROWS, 4 * CHILD_ROWS), :]
        copies.append(pltpu.make_async_copy(source, out_ref.at[z], sems.at[z]))
        copies[z].start()
    for copy in copies:
        copy.wait()


def wanted(where, parts):
    return pl.pallas_call(
        wanted_kernel,
        grid_spec=pltpu.PrefetchScalarGridSpec(
            num_scalar_prefetch=1,
            grid=(1,),
            in_specs=[pl.BlockSpec((4, PART_ROWS, THIRD), lambda i, w: (0, 0, 0))],
            out_specs=pl.BlockSpec(memory_space=pl.ANY),
            scratch_shapes=[pltpu.SemaphoreType.DMA((8,))],
        ),
        out_shape=jax.ShapeDtypeStruct((8, 4 * CHILD_ROWS, THIRD), BF16),
        compiler_params=pltpu.CompilerParams(vmem_limit_bytes=8 * MIB),
        name="wanted",
    )(where, parts)


def on_device(assembled, update, blocks, inverses):
    r, z = lax.axis_index("row"), lax.axis_index("col")
    where = jnp.concatenate([jnp.stack([r, z]).astype(jnp.int32), blocks[0]])

    both, first = first_panel(assembled, inverses)
    columns = lax.all_gather(both, "col", axis=0)
    first, update = lax.optimization_barrier((first, update))
    child = lax.ppermute(update[0], "front", [(i, i ^ 1) for i in range(16)])
    firsts = lax.all_gather(first, "row", axis=0)

    top = firsts[0]
    child, top = lax.optimization_barrier((child, top))
    parts = lax.all_to_all(pack(both, child), "row", 0, 0)
    passed = lax.ppermute(top, "col", [(4, 1), (5, 0), (6, 3), (7, 2)])
    mine = first_relay(where, passed, firsts)
    beside = lax.ppermute(mine, "col", [(i, i ^ 1) for i in range(8)])
    across = lax.ppermute(
        jnp.concatenate([mine, beside]),
        "col",
        [(i, (i + 1) % 8 if i % 2 else (i + 7) % 8) for i in range(8)],
    )
    relay = mine, beside, across
    pieces = wanted(where, parts)
    beside, pieces = lax.optimization_barrier((beside, pieces))
    children = lax.all_to_all(pieces, "col", 0, 0)

    zero, one, two, three, across_groups = products(where, inverses, firsts, parts, columns, relay)
    factor = own_factor(where, assembled, inverses, first, relay)
    two = lax.ppermute(two, "row", [(i, (i + 2) % 4) for i in range(1, 4)])
    one = lax.ppermute(one, "row", [(i, (i + 1) % 4) for i in range(1, 4)])
    three = lax.ppermute(three, "row", [(i, (i + 3) % 4) for i in range(1, 4)])
    pieces = zero, one, two, three, across_groups
    left, lent = join(where, children)
    right = lax.ppermute(lent, "row", [(1, 2), (0, 3)])
    return factor, final(where, assembled, pieces, (left, right))


def solution(mesh):
    return jax.shard_map(
        on_device,
        mesh=mesh,
        in_specs=(
            P("front", ("row", "col"), None),
            P("front", ("row", "col"), None),
            P("front", None),
            P("front", None, None, None),
        ),
        out_specs=(P("front", ("row", "col"), None), P("front", ("row", "col"), None)),
        check_vma=False,
    )
```
